128 devices in a mesh: row: 8 (over y, core), col: 16 (over x, z).
Axes of the slice: x: 4, y: 4, z: 4, core: 2. Of those that a mesh axis runs over, the one named last changes fastest.
Arguments:
- panel: float32 [8192, 512], P('row'), may hold values from -32 to 32, as said below
- trailing: float32 [8192, 8192], P('row', 'col'), may hold values from -86 to 86
Outputs:
- trailing_new: float32 [8192, 8192], P('row', 'col')
- reflectors: float32 [8192, 512], P('row')
The draws below stay inside these ranges and needn't reach their ends.
Inputs may be any that keep to these rules, and one draw needn't show every extreme that they name: The diagonal entries of the panel's top 512 rows are positive and dominate the other entries of their columns in that block.
All inputs are finite; a program needn't handle non-finite values.
Results may differ from the reference program's by a relative error of at most 0.00014.
Values sent between devices are 32-bit elements; how exact they have to be, the bound alone decides.
A program may use at most 128 MiB of HBM per device.

```python
import math
import jax
import jax.numpy as jnp
from jax import lax

NB = 512
N = 8192


def draw_panel(key, part):
    key = jax.random.fold_in(key, 11)
    key_base, key_row, key_col = jax.random.split(key, 3)
    row_scale = jnp.exp(jax.random.uniform(key_row, (N, 1), jnp.float32, 0.0, math.log(10.0)))
    col_scale = jnp.exp(jax.random.uniform(key_col, (1, NB), jnp.float32, 0.0, math.log(4.0)))
    base = jax.random.normal(key_base, (N, NB), jnp.float32)
    base = jnp.clip(base, -6.0, 6.0)
    diagonal = (lax.broadcasted_iota(jnp.int32, (N, NB), 0) == lax.broadcasted_iota(jnp.int32, (N, NB), 1)).astype(jnp.float32)
    return (base * row_scale / math.sqrt(N) + 6.0 * diagonal) * col_scale


def draw_trailing(key, part):
    key = jax.random.fold_in(key, 12)
    key_base, key_scale = jax.random.split(key, 2)
    scales = jnp.exp(jax.random.uniform(key_scale, (N,), jnp.float32, 0.0, math.log(10.0) / 2.0))
    base = jnp.clip(jax.random.normal(key_base, (N, N), jnp.float32), -6.0, 6.0)
    symmetric = (base + base.T) * 0.7071
    return symmetric * scales[:, None] * scales[None, :]


def setup_inputs(seed: int = 0) -> dict:
    arg_keys = jax.random.split(jax.random.key(seed), 3)
    panel = draw_panel(jax.random.fold_in(arg_keys[2], 71), 0)
    trailing = draw_trailing(jax.random.fold_in(arg_keys[2], 71), 0)
    return {"panel": panel, "trailing": trailing}


def mult(left, right):
    return jnp.dot(left, right, precision=lax.Precision.HIGHEST)

def inner_rows(left, right):
    return lax.dot_general(left, right, (((0,), (0,)), ((), ())), precision=lax.Precision.HIGHEST)

def outer_cols(left, right):
    return lax.dot_general(left, right, (((1,), (1,)), ((), ())), precision=lax.Precision.HIGHEST)

def leaf_lu(matrix):
    order = matrix.shape[0]
    positions = jnp.arange(order, dtype=jnp.int32)

    def eliminate(step, current):
        step = step.astype(jnp.int32)
        column = lax.dynamic_index_in_dim(current, step, 1, keepdims=False)
        row_vec = lax.dynamic_index_in_dim(current, step, 0, keepdims=False)
        pivot = lax.dynamic_index_in_dim(row_vec, step, 0, keepdims=False)
        below = positions > step
        factors = jnp.where(below, column / pivot, jnp.zeros_like(column))
        right = jnp.where(below, row_vec, jnp.zeros_like(row_vec))
        current = current - factors[:, None] * right[None, :]
        current = jnp.where(below[:, None] & (positions == step)[None, :], factors[:, None], current)
        return current
    current = lax.fori_loop(0, order, eliminate, matrix)
    lower_unit = jnp.tril(current, -1) + jnp.eye(order, dtype=matrix.dtype)
    return (lower_unit, jnp.triu(current))

def lu_unpivoted(matrix):
    order = matrix.shape[0]
    leaf = min(128, order)
    lower_unit = jnp.zeros_like(matrix)
    upper_factor = jnp.zeros_like(matrix)
    rest = matrix
    for start in range(0, order, leaf):
        lower_one, upper_one = leaf_lu(rest[:leaf, :leaf])
        lower_unit = lower_unit.at[start:start + leaf, start:start + leaf].set(lower_one)
        upper_factor = upper_factor.at[start:start + leaf, start:start + leaf].set(upper_one)
        if start + leaf < order:
            upper_side = jax.scipy.linalg.solve_triangular(lower_one, rest[:leaf, leaf:], lower=True, unit_diagonal=True)
            lower_side = jax.scipy.linalg.solve_triangular(upper_one.T, rest[leaf:, :leaf].T, lower=True).T
            upper_factor = upper_factor.at[start:start + leaf, start + leaf:].set(upper_side)
            lower_unit = lower_unit.at[start + leaf:, start:start + leaf].set(lower_side)
            rest = rest[leaf:, leaf:] - mult(lower_side, upper_side)
    return (lower_unit, upper_factor)

def factor_panel(gram_sum, top_block):
    width = gram_sum.shape[0]
    chol_lower = jnp.linalg.cholesky(gram_sum)
    q_top = jax.scipy.linalg.solve_triangular(chol_lower, top_block.T, lower=True).T
    lower_unit, upper_factor = lu_unpivoted(q_top + jnp.eye(width, dtype=gram_sum.dtype))
    t_factor = jax.scipy.linalg.solve_triangular(lower_unit, upper_factor.T, lower=True, unit_diagonal=True).T
    return (chol_lower, upper_factor, t_factor)

def reference(panel, trailing):
    width = panel.shape[1]
    gram_sum = inner_rows(panel, panel)
    chol_lower, upper_factor, t_factor = factor_panel(gram_sum, panel[:width])
    q_rows = jax.scipy.linalg.solve_triangular(chol_lower, panel.T, lower=True).T
    picks = (jnp.arange(panel.shape[0], dtype=jnp.int32)[:, None] == jnp.arange(width, dtype=jnp.int32)[None, :]).astype(panel.dtype)
    reflectors = jax.scipy.linalg.solve_triangular(upper_factor.T, (q_rows + picks).T, lower=True).T
    scaled = mult(reflectors, t_factor)
    image = mult(trailing, scaled)
    curv = inner_rows(scaled, image)
    update = image - 0.5 * mult(reflectors, curv)
    trailing_new = trailing - outer_cols(reflectors, update) - outer_cols(update, reflectors)
    return (trailing_new, reflectors)
```

```python
import functools
import jax, jax.numpy as jnp
from jax import lax
from jax.experimental import pallas as pl
from jax.experimental.pallas import tpu as pltpu
from jax.sharding import PartitionSpec as P

HI = lax.Precision.HIGHEST
B = 64
NB = 512
NPH = NB // B


def dot(a, b):
    return lax.dot_general(a, b, (((1,), (0,)), ((), ())), precision=HI, preferred_element_type=jnp.float32)


def dot_t(a, b):
    return lax.dot_general(a, b, (((0,), (0,)), ((), ())), precision=HI, preferred_element_type=jnp.float32)


def eliminate(e_ref, count):
    sub = lax.broadcasted_iota(jnp.int32, (8, 128), 0)
    rows = [[e_ref[t, 8 * i : 8 * i + 8, :] for i in range(B // 8)] for t in range(count)]

    def lane(v, k):
        return jnp.broadcast_to(v[:, k : k + 1], (8, 128))

    def row(v, k):
        return jnp.broadcast_to(v[k : k + 1, :], (8, 128))

    for jb in range(B // 8):
        full = [rows[t][jb] for t in range(count)]
        cols = [[lane(full[t], 8 * jb + m) for m in range(8)] for t in range(count)]
        kept = list(full)
        for m in range(8):
            for t in range(count):
                here = sub == m
                col = cols[t][m]
                rp = 1.0 / row(col, m)
                if m:
                    kept[t] = jnp.where(here, full[t], kept[t])
                scaled = row(full[t], m) * rp
                full[t] = jnp.where(here, scaled, full[t] - col * scaled)
                for k in range(m + 1, 8):
                    scaled = row(cols[t][k], m) * rp
                    cols[t][k] = jnp.where(here, scaled, cols[t][k] - col * scaled)
        for t in range(count):
            rows[t][jb] = kept[t]
            spread = [row(full[t], m) for m in range(8)]
            for i in range(jb + 1, B // 8):
                terms = [lane(rows[t][i], 8 * jb + m) * spread[m] for m in range(8)]
                while len(terms) > 1:
                    terms = [terms[k] + terms[k + 1] for k in range(0, len(terms), 2)]
                rows[t][i] = rows[t][i] - terms[0]
    for t in range(count):
        for i in range(B // 8):
            e_ref[t, 8 * i : 8 * i + 8, :] = rows[t][i]


def factor_kernel(g_ref, a1_ref, r_ref, rit_ref, lui_ref, mi_ref, x_ref, s_ref, e_ref):
    r_i = lax.broadcasted_iota(jnp.int32, (B, B), 0)
    c_i = lax.broadcasted_iota(jnp.int32, (B, B), 1)
    eye = (r_i == c_i).astype(jnp.float32)
    x_ref[...] = g_ref[...]
    s_ref[...] = a1_ref[...]
    r_ref[...] = jnp.zeros_like(r_ref)
    rit_ref[...] = jnp.zeros_like(rit_ref)
    lui_ref[...] = jnp.zeros_like(lui_ref)
    mi_ref[...] = jnp.zeros_like(mi_ref)
    for t in range(3):
        e_ref[t, :, :B] = eye
        e_ref[t, :, B:] = eye

    def diag(v):
        return jnp.sum(jnp.where(r_i == c_i, v, 0.0), axis=1, keepdims=True)

    def pre(p):
        a, b = p * B, (p + 1) * B
        if p < NPH:
            e_ref[0, :, :B] = x_ref[a:b, a:b]
            e_ref[0, :, B:] = eye
        if p > 0:
            a, b = a - B, b - B
            block = s_ref[a:b, a:b]
            e_ref[1, :, :B] = block
            e_ref[1, :, B:] = eye
            e_ref[2, :, :B] = block.T
            e_ref[2, :, B:] = eye

    def post(p):
        a, b = p * B, (p + 1) * B
        if p < NPH:
            left = e_ref[0, :, :B]
            rs = lax.rsqrt(diag(left))
            linv = rs * e_ref[0, :, B:]
            rpp = jnp.where(r_i <= c_i, rs * left, 0.0)
            r_ref[a:b, a:b] = rpp
            rit_ref[a:b, a:b] = linv
            if p:
                rit_ref[a:b, :a] = dot(linv, rit_ref[a:b, :a])
            s_ref[a:b, a:b] += rpp
            if b < NB:
                rrow = dot(linv, x_ref[a:b, b:])
                r_ref[a:b, b:] = rrow
                s_ref[a:b, b:] += rrow
                x_ref[b:, b:] -= dot_t(rrow, rrow)
                rit_ref[b:, :b] -= dot_t(rrow, rit_ref[a:b, :b])
        if p > 0:
            a, b = a - B, b - B
            lui = e_ref[1, :, B:]
            mit = (1.0 / diag(e_ref[2, :, :B])) * e_ref[2, :, B:]
            mi = mit.T
            lui_ref[a:b, a:b] = lui
            mi_ref[a:b, a:b] = mi
            if a:
                lui_ref[a:b, :a] = dot(lui, lui_ref[a:b, :a])
                mi_ref[:a, a:b] = dot(mi_ref[:a, a:b], mi)
            if b < NB:
                mrow = dot(lui, s_ref[a:b, b:])
                lucol = dot(s_ref[b:, a:b], mi)
                s_ref[b:, b:] -= dot(lucol, mrow)
                lui_ref[b:, :b] -= dot(lucol, lui_ref[a:b, :b])
                mi_ref[:b, b:] -= dot(mi_ref[:b, a:b], mrow)

    def phase(ph, carry):
        for p in range(NPH + 1):
            pl.when(ph == p)(functools.partial(pre, p))
        eliminate(e_ref, 3)
        for p in range(NPH + 1):
            pl.when(ph == p)(functools.partial(post, p))
        return carry

    lax.fori_loop(0, NPH + 1, phase, 0)


def factor(g, a1):
    sq = jax.ShapeDtypeStruct((NB, NB), jnp.float32)
    vm = pl.BlockSpec(memory_space=pltpu.VMEM)
    return pl.pallas_call(
        factor_kernel,
        out_shape=[sq] * 4,
        in_specs=[vm] * 2,
        out_specs=[vm] * 4,
        scratch_shapes=[
            pltpu.VMEM((NB, NB), jnp.float32),
            pltpu.VMEM((NB, NB), jnp.float32),
            pltpu.VMEM((3, B, 2 * B), jnp.float32),
        ],
        compiler_params=pltpu.CompilerParams(vmem_limit_bytes=50 * 1024 * 1024),
        name="factor",
    )(g, a1)


def mult(left, right):
    return jnp.dot(left, right, precision=lax.Precision.HIGHEST)


def inner_rows(left, right):
    return lax.dot_general(left, right, (((0,), (0,)), ((), ())), precision=lax.Precision.HIGHEST)


def outer_cols(left, right):
    return lax.dot_general(left, right, (((1,), (1,)), ((), ())), precision=lax.Precision.HIGHEST)


def from_root(block, axis, source):
    block = jnp.where(lax.axis_index(axis) == source, block, jnp.zeros_like(block))
    return lax.psum(block, axis)


def on_device(panel, trailing):
    rows_dev = panel.shape[0]
    col_rows = trailing.shape[1]
    fanout = lax.axis_size("col") // lax.axis_size("row")
    row_index = lax.axis_index("row")
    col_index = lax.axis_index("col")
    owner_row = col_index // fanout
    place = col_index % fanout * col_rows
    gram = inner_rows(panel, panel)
    top = jnp.where(row_index == 0, panel[:NB], jnp.zeros((NB, NB), jnp.float32))
    gram, top = lax.psum((gram, top), "row")
    panel_cols = from_root(lax.dynamic_slice_in_dim(panel, place, col_rows, 0), "row", owner_row)
    r_up, rit, lui, mi = factor(gram, top)
    k2 = mult(rit.T, lui.T)
    shifted = panel.at[:NB].add(jnp.where(row_index == 0, r_up, jnp.zeros_like(r_up)))
    shifted_cols = panel_cols + jnp.where(col_index == 0, r_up, jnp.zeros_like(r_up))
    reflectors = mult(shifted, mi)
    scaled_rows = mult(shifted, k2)
    vec_cols = mult(shifted_cols, mi)
    scaled_cols = mult(shifted_cols, k2)
    image_rows = lax.psum(mult(trailing, scaled_cols), "col")
    curv = lax.psum(inner_rows(scaled_rows, image_rows), "row")
    update_rows = image_rows - 0.5 * mult(reflectors, curv)
    upd_slice = lax.dynamic_slice_in_dim(update_rows, place, col_rows, 0)
    update_cols = from_root(upd_slice, "row", owner_row)
    trailing_new = (
        trailing - outer_cols(reflectors, update_cols) - outer_cols(update_rows, vec_cols)
    )
    return (trailing_new, reflectors)


def solution(mesh):
    return jax.shard_map(
        on_device,
        mesh=mesh,
        in_specs=(P("row", None), P("row", "col")),
        out_specs=(P("row", "col"), P("row", None)),
        check_vma=False,
    )
```

```python
import functools
import jax, jax.numpy as jnp
from jax import lax
from jax.experimental import pallas as pl
from jax.experimental.pallas import tpu as pltpu
from jax.sharding import PartitionSpec as P

HI = lax.Precision.HIGHEST
MESH = pl.DeviceIdType.MESH
B = 64
NB = 512
NPH = NB // B
T = 128
PAIRS = [(i, j) for i in range(NB // T) for j in range(i, NB // T)]
PIECE = len(PAIRS) * T // 8


def dot(a, b):
    return lax.dot_general(a, b, (((1,), (0,)), ((), ())), precision=HI, preferred_element_type=jnp.float32)


def dot_t(a, b):
    return lax.dot_general(a, b, (((0,), (0,)), ((), ())), precision=HI, preferred_element_type=jnp.float32)


def eliminate(e_ref, count):
    sub = lax.broadcasted_iota(jnp.int32, (8, 128), 0)
    rows = [[e_ref[t, 8 * i : 8 * i + 8, :] for i in range(B // 8)] for t in range(count)]

    def lane(v, k):
        return jnp.broadcast_to(v[:, k : k + 1], (8, 128))

    def row(v, k):
        return jnp.broadcast_to(v[k : k + 1, :], (8, 128))

    for jb in range(B // 8):
        full = [rows[t][jb] for t in range(count)]
        cols = [[lane(full[t], 8 * jb + m) for m in range(8)] for t in range(count)]
        kept = list(full)
        for m in range(8):
            for t in range(count):
                here = sub == m
                col = cols[t][m]
                rp = 1.0 / row(col, m)
                if m:
                    kept[t] = jnp.where(here, full[t], kept[t])
                scaled = row(full[t], m) * rp
                full[t] = jnp.where(here, scaled, full[t] - col * scaled)
                for k in range(m + 1, 8):
                    scaled = row(cols[t][k], m) * rp
                    cols[t][k] = jnp.where(here, scaled, cols[t][k] - col * scaled)
        for t in range(count):
            rows[t][jb] = kept[t]
            spread = [row(full[t], m) for m in range(8)]
            for i in range(jb + 1, B // 8):
                terms = [lane(rows[t][i], 8 * jb + m) * spread[m] for m in range(8)]
                while len(terms) > 1:
                    terms = [terms[k] + terms[k + 1] for k in range(0, len(terms), 2)]
                rows[t][i] = rows[t][i] - terms[0]
    for t in range(count):
        for i in range(B // 8):
            e_ref[t, 8 * i : 8 * i + 8, :] = rows[t][i]


def remote(src, dst, sends, recvs, n, device):
    return pltpu.make_async_remote_copy(
        src_ref=src, dst_ref=dst, send_sem=sends.at[n], recv_sem=recvs.at[n],
        device_id=device, device_id_type=MESH,
    )


def gather_kernel_part(panel_ref, x_ref, s_ref, gp, other, half, parts, total, top, sends, recvs):
    r, c = lax.axis_index("row"), lax.axis_index("col")
    y, k = lax.div(r, 2), lax.rem(r, 2)
    x, z = lax.div(c, 4), lax.rem(c, 4)
    ys = [lax.rem(y + d, 4) for d in range(1, 4)]
    mate = (2 * y + 1 - k, c)
    y_mates = [(2 * v + k, c) for v in ys]
    y_cross = [(2 * v + 1 - k, c) for v in ys]
    x_mates = [(r, lax.rem(x + d, 4) * 4 + z) for d in range(1, 4)]
    z_mates = [(r, x * 4 + lax.rem(z + d, 4)) for d in range(1, 4)]
    peers = [mate] + y_mates + y_cross + x_mates + z_mates
    barrier = pltpu.get_barrier_semaphore()
    for peer in peers:
        pl.semaphore_signal(barrier, inc=1, device_id=peer, device_id_type=MESH)

    for i in range(NB // T):
        strip = dot_t(panel_ref[:, i * T : (i + 1) * T], panel_ref[:, i * T :])
        for j in range(i, NB // T):
            n = PAIRS.index((i, j)) * T
            done = 0
            while done < T:
                q, o = divmod(n + done, PIECE)
                m = min(T - done, PIECE - o)
                gp[q, o : o + m, :] = strip[done : done + m, (j - i) * T : (j - i + 1) * T]
                done += m
    pl.semaphore_wait(barrier, len(peers))

    first = remote(gp.at[pl.ds(4 * (1 - k), 4)], other, sends, recvs, 0, mate)
    first.start()

    @pl.when(r == 0)
    def _():
        out = []
        for n, peer in enumerate([(1, c)] + [(2 * v + q, c) for v in range(1, 4) for q in range(2)]):
            q = 1 if n == 0 else (n - 1) % 2
            src = panel_ref.at[pl.ds(pl.multiple_of(32 * c + 16 * q, 16), 16)]
            place = x + 4 * z if q == 0 else z + 4 * x
            cp = pltpu.make_async_remote_copy(
                src_ref=src, dst_ref=top.at[q, place], send_sem=sends.at[16 + n], recv_sem=recvs.at[1],
                device_id=peer, device_id_type=MESH)
            cp.start()
            out.append(cp)
        top[0, x + 4 * z] = panel_ref[pl.ds(pl.multiple_of(32 * c, 16), 16), :]
        for cp in out:
            cp.wait_send()

    first.wait()
    half[...] = gp[pl.ds(4 * k, 4)] + other[...]
    second = []
    for d in range(3):
        cp = remote(half.at[ys[d]], parts.at[d], sends, recvs, 2 + d, y_mates[d])
        cp.start()
        second.append(cp)

    mine = jnp.where(k == 0, x + 4 * z, z + 4 * x)

    @pl.when(r > 0)
    def _():
        remote(top.at[k, mine], top.at[k, mine], sends, recvs, 1, mate).wait_recv()

    def spread_top(base, src, peers_0, peers_1):
        cps = []
        for d in range(3):
            peer = (r, jnp.where(k == 0, peers_0[d][1], peers_1[d][1]))
            cp = remote(src, src, sends, recvs, base + d, peer)
            cp.start()
            cps.append(cp)
        return cps

    third = spread_top(5, top.at[k, mine], x_mates, z_mates)
    for cp in second:
        cp.wait()
    total[4 * k + y] = (half[y] + parts[0]) + (parts[1] + parts[2])
    fourth = []
    for d in range(3):
        cp = remote(total.at[4 * k + y], total.at[4 * k + y], sends, recvs, 8 + d, y_mates[d])
        cp.start()
        fourth.append(cp)
    for cp in third:
        cp.wait()
    group = pl.ds(4 * jnp.where(k == 0, z, x), 4)
    fifth = spread_top(11, top.at[k, group], z_mates, x_mates)
    for cp in fourth:
        cp.wait()
    sixth = remote(total.at[pl.ds(4 * k, 4)], total.at[pl.ds(4 * k, 4)], sends, recvs, 14, mate)
    sixth.start()
    for cp in fifth:
        cp.wait()
    seventh = remote(top.at[k], top.at[k], sends, recvs, 15, mate)
    seventh.start()
    sixth.wait()
    for n, (i, j) in enumerate(PAIRS):
        done = 0
        while done < T:
            q, o = divmod(n * T + done, PIECE)
            m = min(T - done, PIECE - o)
            x_ref[i * T + done : i * T + done + m, j * T : (j + 1) * T] = total[q, o : o + m, :]
            done += m
    seventh.wait()
    for a in range(4):
        for b in range(4):
            s_ref[32 * (4 * a + b) : 32 * (4 * a + b) + 16, :] = top[0, a + 4 * b]
            s_ref[32 * (4 * a + b) + 16 : 32 * (4 * a + b) + 32, :] = top[1, b + 4 * a]


def factor_kernel(panel_ref, r_ref, rit_ref, lui_ref, mi_ref, x_ref, s_ref, e_ref, gp, other, half, parts, total, top, sends, recvs):
    gather_kernel_part(panel_ref, x_ref, s_ref, gp, other, half, parts, total, top, sends, recvs)
    r_i = lax.broadcasted_iota(jnp.int32, (B, B), 0)
    c_i = lax.broadcasted_iota(jnp.int32, (B, B), 1)
    eye = (r_i == c_i).astype(jnp.float32)
    r_ref[...] = jnp.zeros_like(r_ref)
    rit_ref[...] = jnp.zeros_like(rit_ref)
    lui_ref[...] = jnp.zeros_like(lui_ref)
    mi_ref[...] = jnp.zeros_like(mi_ref)
    for t in range(3):
        e_ref[t, :, :B] = eye
        e_ref[t, :, B:] = eye

    def diag(v):
        return jnp.sum(jnp.where(r_i == c_i, v, 0.0), axis=1, keepdims=True)

    def pre(p):
        a, b = p * B, (p + 1) * B
        if p < NPH:
            block = x_ref[a:b, a:b]
            e_ref[0, :, :B] = jnp.where(r_i <= c_i, block, block.T)
            e_ref[0, :, B:] = eye
        if p > 0:
            a, b = a - B, b - B
            block = s_ref[a:b, a:b]
            e_ref[1, :, :B] = block
            e_ref[1, :, B:] = eye
            e_ref[2, :, :B] = block.T
            e_ref[2, :, B:] = eye

    def post(p):
        a, b = p * B, (p + 1) * B
        if p < NPH:
            left = e_ref[0, :, :B]
            rs = lax.rsqrt(diag(left))
            linv = rs * e_ref[0, :, B:]
            rpp = jnp.where(r_i <= c_i, rs * left, 0.0)
            r_ref[a:b, a:b] = rpp
            rit_ref[a:b, a:b] = linv
            if p:
                rit_ref[a:b, :a] = dot(linv, rit_ref[a:b, :a])
            s_ref[a:b, a:b] += rpp
            if b < NB:
                rrow = dot(linv, x_ref[a:b, b:])
                r_ref[a:b, b:] = rrow
                s_ref[a:b, b:] += rrow
                x_ref[b:, b:] -= dot_t(rrow, rrow)
                rit_ref[b:, :b] -= dot_t(rrow, rit_ref[a:b, :b])
        if p > 0:
            a, b = a - B, b - B
            lui = e_ref[1, :, B:]
            mit = (1.0 / diag(e_ref[2, :, :B])) * e_ref[2, :, B:]
            mi = mit.T
            lui_ref[a:b, a:b] = lui
            mi_ref[a:b, a:b] = mi
            if a:
                lui_ref[a:b, :a] = dot(lui, lui_ref[a:b, :a])
                mi_ref[:a, a:b] = dot(mi_ref[:a, a:b], mi)
            if b < NB:
                mrow = dot(lui, s_ref[a:b, b:])
                lucol = dot(s_ref[b:, a:b], mi)
                s_ref[b:, b:] -= dot(lucol, mrow)
                lui_ref[b:, :b] -= dot(lucol, lui_ref[a:b, :b])
                mi_ref[:b, b:] -= dot(mi_ref[:b, a:b], mrow)

    def phase(ph, carry):
        for p in range(NPH + 1):
            pl.when(ph == p)(functools.partial(pre, p))
        eliminate(e_ref, 3)
        for p in range(NPH + 1):
            pl.when(ph == p)(functools.partial(post, p))
        return carry

    lax.fori_loop(0, NPH + 1, phase, 0)


def factor(panel):
    sq = jax.ShapeDtypeStruct((NB, NB), jnp.float32)
    vm = pl.BlockSpec(memory_space=pltpu.VMEM)
    f32 = jnp.float32
    return pl.pallas_call(
        factor_kernel,
        out_shape=[sq] * 4,
        in_specs=[vm],
        out_specs=[vm] * 4,
        scratch_shapes=[
            pltpu.VMEM((NB, NB), f32),
            pltpu.VMEM((NB, NB), f32),
            pltpu.VMEM((3, B, 2 * B), f32),
            pltpu.VMEM((8, PIECE, T), f32),
            pltpu.VMEM((4, PIECE, T), f32),
            pltpu.VMEM((4, PIECE, T), f32),
            pltpu.VMEM((3, PIECE, T), f32),
            pltpu.VMEM((8, PIECE, T), f32),
            pltpu.VMEM((2, 16, 16, NB), f32),
            pltpu.SemaphoreType.DMA((24,)),
            pltpu.SemaphoreType.DMA((16,)),
        ],
        compiler_params=pltpu.CompilerParams(
            vmem_limit_bytes=50 * 1024 * 1024, collective_id=0, has_side_effects=True),
        name="factor",
    )(panel)


def mult(left, right):
    return jnp.dot(left, right, precision=lax.Precision.HIGHEST)


def inner_rows(left, right):
    return lax.dot_general(left, right, (((0,), (0,)), ((), ())), precision=lax.Precision.HIGHEST)


def outer_cols(left, right):
    return lax.dot_general(left, right, (((1,), (1,)), ((), ())), precision=lax.Precision.HIGHEST)


def from_root(block, axis, source):
    block = jnp.where(lax.axis_index(axis) == source, block, jnp.zeros_like(block))
    return lax.psum(block, axis)


def on_device(panel, trailing):
    rows_dev = panel.shape[0]
    col_rows = trailing.shape[1]
    fanout = lax.axis_size("col") // lax.axis_size("row")
    row_index = lax.axis_index("row")
    col_index = lax.axis_index("col")
    owner_row = col_index // fanout
    place = col_index % fanout * col_rows
    panel_cols = from_root(lax.dynamic_slice_in_dim(panel, place, col_rows, 0), "row", owner_row)
    r_up, rit, lui, mi = factor(panel)
    k2 = mult(rit.T, lui.T)
    shifted = panel.at[:NB].add(jnp.where(row_index == 0, r_up, jnp.zeros_like(r_up)))
    shifted_cols = panel_cols + jnp.where(col_index == 0, r_up, jnp.zeros_like(r_up))
    reflectors = mult(shifted, mi)
    scaled_rows = mult(shifted, k2)
    vec_cols = mult(shifted_cols, mi)
    scaled_cols = mult(shifted_cols, k2)
    image_rows = lax.psum(mult(trailing, scaled_cols), "col")
    curv = lax.psum(inner_rows(scaled_rows, image_rows), "row")
    update_rows = image_rows - 0.5 * mult(reflectors, curv)
    upd_slice = lax.dynamic_slice_in_dim(update_rows, place, col_rows, 0)
    update_cols = from_root(upd_slice, "row", owner_row)
    trailing_new = (
        trailing - outer_cols(reflectors, update_cols) - outer_cols(update_rows, vec_cols)
    )
    return (trailing_new, reflectors)


def solution(mesh):
    return jax.shard_map(
        on_device,
        mesh=mesh,
        in_specs=(P("row", None), P("row", "col")),
        out_specs=(P("row", "col"), P("row", None)),
        check_vma=False,
    )
```

```python
import functools
import jax, jax.numpy as jnp
from jax import lax
from jax.experimental import pallas as pl
from jax.experimental.pallas import tpu as pltpu
from jax.sharding import PartitionSpec as P

HI = lax.Precision.HIGHEST
MESH = pl.DeviceIdType.MESH
B = 64
NB = 512
NPH = NB // B
T = 128
PAIRS = [(i, j) for i in range(NB // T) for j in range(i, NB // T)]
PIECE = len(PAIRS) * T // 8


def dot(a, b):
    return lax.dot_general(a, b, (((1,), (0,)), ((), ())), precision=HI, preferred_element_type=jnp.float32)


def dot_t(a, b):
    return lax.dot_general(a, b, (((0,), (0,)), ((), ())), precision=HI, preferred_element_type=jnp.float32)


def split(a):
    hi = a.astype(jnp.bfloat16)
    return hi, (a - hi.astype(jnp.float32)).astype(jnp.bfloat16)


def dot3(a, b, dims=((1,), (0,))):
    (ah, al), (bh, bl) = (v if isinstance(v, tuple) else split(v) for v in (a, b))

    def one(p, q):
        return lax.dot_general(p, q, (dims, ((), ())), preferred_element_type=jnp.float32)

    return one(ah, bh) + (one(ah, bl) + one(al, bh))


NT = ((1,), (1,))
TN = ((0,), (0,))


def eliminate(e_ref, count):
    sub = lax.broadcasted_iota(jnp.int32, (8, 128), 0)
    rows = [[e_ref[t, 8 * i : 8 * i + 8, :] for i in range(B // 8)] for t in range(count)]

    def lane(v, k):
        return jnp.broadcast_to(v[:, k : k + 1], (8, 128))

    def row(v, k):
        return jnp.broadcast_to(v[k : k + 1, :], (8, 128))

    for jb in range(B // 8):
        full = [rows[t][jb] for t in range(count)]
        cols = [[lane(full[t], 8 * jb + m) for m in range(8)] for t in range(count)]
        kept = list(full)
        for m in range(8):
            for t in range(count):
                here = sub == m
                col = cols[t][m]
                rp = 1.0 / row(col, m)
                if m:
                    kept[t] = jnp.where(here, full[t], kept[t])
                scaled = row(full[t], m) * rp
                full[t] = jnp.where(here, scaled, full[t] - col * scaled)
                for k in range(m + 1, 8):
                    scaled = row(cols[t][k], m) * rp
                    cols[t][k] = jnp.where(here, scaled, cols[t][k] - col * scaled)
        for t in range(count):
            rows[t][jb] = kept[t]
            spread = [row(full[t], m) for m in range(8)]
            for i in range(jb + 1, B // 8):
                terms = [lane(rows[t][i], 8 * jb + m) * spread[m] for m in range(8)]
                while len(terms) > 1:
                    terms = [terms[k] + terms[k + 1] for k in range(0, len(terms), 2)]
                rows[t][i] = rows[t][i] - terms[0]
    for t in range(count):
        for i in range(B // 8):
            e_ref[t, 8 * i : 8 * i + 8, :] = rows[t][i]


def remote(src, dst, sends, recvs, n, device):
    return pltpu.make_async_remote_copy(
        src_ref=src, dst_ref=dst, send_sem=sends.at[n], recv_sem=recvs.at[n],
        device_id=device, device_id_type=MESH,
    )


class Sum:
    def __init__(self, bufs, sems, base, here):
        self.gp, self.other, self.half, self.parts, self.total = bufs
        self.sems, self.base, self.here = sems, base, here

    def fill(self, strip_of):
        for i in range(NB // T):
            strip = strip_of(i)
            for j in range(i, NB // T):
                n = PAIRS.index((i, j)) * T
                done = 0
                while done < T:
                    q, o = divmod(n + done, PIECE)
                    m = min(T - done, PIECE - o)
                    self.gp[q, o : o + m, :] = strip[done : done + m, (j - i) * T : (j - i + 1) * T]
                    done += m

    def first(self):
        k, mate = self.here["k"], self.here["mate"]
        return [remote(self.gp.at[pl.ds(4 * (1 - k), 4)], self.other, *self.sems, self.base, mate)]

    def add_pair(self):
        self.half[...] = self.gp[pl.ds(4 * self.here["k"], 4)] + self.other[...]

    def second(self):
        h = self.here
        return [
            remote(self.half.at[h["ys"][d]], self.parts.at[d], *self.sems, self.base + 1 + d, h["y_mates"][d])
            for d in range(3)
        ]

    def add_ring(self):
        k, y = self.here["k"], self.here["y"]
        self.total[4 * k + y] = (self.half[y] + self.parts[0]) + (self.parts[1] + self.parts[2])

    def third(self):
        h = self.here
        slot = self.total.at[4 * h["k"] + h["y"]]
        return [remote(slot, slot, *self.sems, self.base + 4 + d, h["y_mates"][d]) for d in range(3)]

    def fourth(self):
        group = self.total.at[pl.ds(4 * self.here["k"], 4)]
        return [remote(group, group, *self.sems, self.base + 7, self.here["mate"])]

    def unpack(self, store):
        for n, (i, j) in enumerate(PAIRS):
            done = 0
            while done < T:
                q, o = divmod(n * T + done, PIECE)
                m = min(T - done, PIECE - o)
                store(i * T + done, m, j * T, self.total[q, o : o + m, :])
                done += m


def start(copies):
    for cp in copies:
        cp.start()


def wait(copies):
    for cp in copies:
        cp.wait()


def step_kernel(
    panel_ref, trail_ref, out_ref, vec_ref,
    r_ref, rit_ref, lui_ref, mi_ref, x_ref, s_ref, e_ref,
    g0, g1, g2, g3, g4, c0, c1, c2, c3, c4,
    top, zp, zo, zh, zparts, zc, zs, xs, az0, az1, ax0, ax1, pc, qc,
    k2t, img, wr, vc, yct, cc, sends, recvs,
):
    r, c = lax.axis_index("row"), lax.axis_index("col")
    y, k = lax.div(r, 2), lax.rem(r, 2)
    x, z = lax.div(c, 4), lax.rem(c, 4)
    ys = [lax.rem(y + d, 4) for d in range(1, 4)]
    mate = (2 * y + 1 - k, c)
    y_mates = [(2 * v + k, c) for v in ys]
    y_cross = [(2 * v + 1 - k, c) for v in ys]
    x_mates = [(r, lax.rem(x + d, 4) * 4 + z) for d in range(1, 4)]
    z_mates = [(r, x * 4 + lax.rem(z + d, 4)) for d in range(1, 4)]
    peers = [mate] + y_mates + y_cross + x_mates + z_mates
    sems = (sends, recvs)
    here = {"k": k, "y": y, "ys": ys, "mate": mate, "y_mates": y_mates}
    to_r, to_c = lax.div(c, 2), 8 * lax.rem(c, 2) + r
    from_r, from_c = lax.rem(c, 8), 2 * r + lax.div(c, 8)
    fixed = (to_r == r) & (to_c == c)

    barrier = pltpu.get_barrier_semaphore()
    for peer in peers:
        pl.semaphore_signal(barrier, inc=1, device_id=peer, device_id_type=MESH)

    @pl.when(jnp.logical_not(fixed))
    def _():
        pl.semaphore_signal(barrier, inc=1, device_id=(from_r, from_c), device_id_type=MESH)

    @pl.when((x > 0) & (z > 0))
    def _():
        pl.semaphore_signal(barrier, inc=1, device_id=(r, 0), device_id_type=MESH)

    gram = Sum((g0, g1, g2, g3, g4), sems, 0, here)
    curv = Sum((c0, c1, c2, c3, c4), sems, 8, here)
    TOP, ZRS, ZAG, PERM, XSC, AXA, AXB, AZA, AZB, PAN, QQ = 16, 24, 28, 32, 33, 34, 40, 46, 52, 58, 63
    FAN = 70

    gram.fill(lambda i: dot_t(panel_ref[:, i * T : (i + 1) * T], panel_ref[:, i * T :]))

    pl.semaphore_wait(barrier, len(peers) + jnp.where(c == 0, 9, 0) + jnp.where(fixed, 0, 1))

    def top_out():
        out = []
        for n, peer in enumerate([(1, c)] + [(2 * v + q, c) for v in range(1, 4) for q in range(2)]):
            q = 1 if n == 0 else (n - 1) % 2
            place = x + 4 * z if q == 0 else z + 4 * x
            out.append(pltpu.make_async_remote_copy(
                src_ref=panel_ref.at[pl.ds(pl.multiple_of(32 * c + 16 * q, 16), 16)],
                dst_ref=top.at[q, place], send_sem=sends.at[FAN + n], recv_sem=recvs.at[TOP],
                device_id=peer, device_id_type=MESH))
        return out

    mine = jnp.where(k == 0, x + 4 * z, z + 4 * x)

    def top_spread(base, src, peers_0, peers_1):
        return [
            remote(src, src, sends, recvs, base + d, (r, jnp.where(k == 0, peers_0[d][1], peers_1[d][1])))
            for d in range(3)
        ]

    top_a = lambda: top_spread(TOP + 1, top.at[k, mine], x_mates, z_mates)
    top_b = lambda: top_spread(TOP + 4, top.at[k, pl.ds(4 * jnp.where(k == 0, z, x), 4)], z_mates, x_mates)
    top_c = lambda: [remote(top.at[k], top.at[k], sends, recvs, TOP + 7, mate)]

    def first_cols_out():
        return [
            pltpu.make_async_remote_copy(
                src_ref=trail_ref.at[pl.ds(64 * n, 64)], dst_ref=xs, send_sem=sends.at[FAN + 7 + n],
                recv_sem=recvs.at[XSC], device_id=(r, n), device_id_type=MESH)
            for n in range(1, 16)
        ]

    def gather_a(src, h0, h1, base):
        return [remote(src.at[pl.ds(0, 32)], h0.at[4 * z + x], sends, recvs, base + d, x_mates[d]) for d in range(3)] + [
            remote(src.at[pl.ds(32, 32)], h1.at[4 * x + z], sends, recvs, base + 3 + d, z_mates[d]) for d in range(3)]

    def gather_own(src, h0, h1):
        h0[4 * z + x] = src[0:32, :]
        h1[4 * x + z] = src[32:64, :]

    def gather_b(h0, h1, base):
        g0_, g1_ = h0.at[pl.ds(4 * z, 4)], h1.at[pl.ds(4 * x, 4)]
        return [remote(g0_, g0_, sends, recvs, base + d, z_mates[d]) for d in range(3)] + [
            remote(g1_, g1_, sends, recvs, base + 3 + d, x_mates[d]) for d in range(3)]

    def z_first():
        return [remote(zp.at[pl.ds(4 * (1 - k), 4)], zo, sends, recvs, ZRS, mate)]

    def z_second():
        return [remote(zh.at[ys[d]], zparts.at[d], sends, recvs, ZRS + 1 + d, y_mates[d]) for d in range(3)]

    def z_third():
        slot = zc.at[y, k]
        return [remote(slot, slot, sends, recvs, ZAG + d, y_mates[d]) for d in range(3)]

    def z_fourth():
        return [remote(zc.at[:, k], zc.at[:, k], sends, recvs, ZAG + 3, mate)]

    def z_move():
        return remote(zc.at[y, k], zs, sends, recvs, PERM, (to_r, to_c))

    def block_first(src_half, dst, base, at_y, at_k):
        return remote(src_half, dst.at[1 - at_k], sends, recvs, base, mate)

    def block_second(dst, base, at_y):
        return [remote(dst.at[k], dst.at[k], sends, recvs, base + 1 + d, y_mates[d]) for d in range(3)]

    def block_third(dst, base):
        return [remote(dst.at[k], dst.at[k], sends, recvs, base + 4, mate)]

    pan_y, pan_k = x, lax.div(z, 2)
    pan_row = 512 * lax.rem(c, 2)

    def pan_src(h):
        return panel_ref.at[pl.ds(pl.multiple_of(pan_row + 256 * h, 256), 256)]

    start(gram.first())
    pl.when(r == 0)(lambda: start(top_out()))
    pl.when(c == 0)(lambda: start(first_cols_out()))

    @pl.when((y == pan_y) & (k == pan_k))
    def _():
        block_first(pan_src(1 - pan_k), pc, PAN, pan_y, pan_k).start()
        pc[k] = panel_ref[pl.ds(pl.multiple_of(pan_row + 256 * pan_k, 256), 256), :]

    @pl.when(r == 0)
    def _():
        block_first(trail_ref.at[pl.ds(256, 256)], qc, QQ, 0, 0).start()
        qc[0] = trail_ref[0:256, :]
        top[0, x + 4 * z] = panel_ref[pl.ds(pl.multiple_of(32 * c, 32), 16), :]

    @pl.when(c == 0)
    def _():
        xs[...] = trail_ref[0:64, :]

    wait(gram.first())
    gram.add_pair()
    start(gram.second())

    for half in range(2):
        acc = None
        for q in range(4):
            left = trail_ref[256 * q : 256 * (q + 1), 256 * half : 256 * (half + 1)].T
            term = dot3(left, panel_ref[256 * q : 256 * (q + 1), :])
            acc = term if acc is None else acc + term
        for q in range(4):
            s = 4 * half + q
            zp[4 * (s % 2) + s // 2] = acc[64 * q : 64 * (q + 1), :]
    start(z_first())

    @pl.when(r > 0)
    def _():
        remote(top.at[k, mine], top.at[k, mine], sends, recvs, TOP, mate).wait_recv()

    start(top_a())
    wait(gram.second())
    gram.add_ring()
    start(gram.third())
    wait(top_a())
    start(top_b())
    wait(z_first())
    zh[...] = zp[pl.ds(4 * k, 4)] + zo[...]
    wait(gram.third())
    start(gram.fourth())
    start(z_second())
    wait(top_b())
    start(top_c())
    wait(gram.fourth())

    def put(i, m, j, v):
        x_ref[i : i + m, j : j + T] = v

    gram.unpack(put)
    wait(top_c())
    for a in range(4):
        for b in range(4):
            s_ref[32 * (4 * a + b) : 32 * (4 * a + b) + 16, :] = top[0, a + 4 * b]
            s_ref[32 * (4 * a + b) + 16 : 32 * (4 * a + b) + 32, :] = top[1, b + 4 * a]
    pl.when(r == 0)(lambda: [cp.wait_send() for cp in top_out()] and None)

    def hook0():
        @pl.when(c > 0)
        def _():
            remote(xs, xs, sends, recvs, XSC, mate).wait_recv()

        gather_own(xs, ax0, ax1)
        start(gather_a(xs, ax0, ax1, AXA))
        wait(z_second())
        zc[y, k] = (zh[y] + zparts[0]) + (zparts[1] + zparts[2])
        start(z_third())

        @pl.when(fixed)
        def _():
            zs[...] = zc[y, k]

        @pl.when(jnp.logical_not(fixed))
        def _():
            z_move().start()

    def hook1():
        wait(gather_a(xs, ax0, ax1, AXA))
        start(gather_b(ax0, ax1, AXB))
        wait(z_third())
        start(z_fourth())

        @pl.when(y == pan_y)
        def _():
            @pl.when(k != pan_k)
            def _():
                block_first(pan_src(k), pc, PAN, pan_y, pan_k).wait_recv()

            start(block_second(pc, PAN, pan_y))

        @pl.when(y == 0)
        def _():
            @pl.when(k != 0)
            def _():
                block_first(trail_ref.at[pl.ds(256, 256)], qc, QQ, 0, 0).wait_recv()

            start(block_second(qc, QQ, 0))

    def hook2():
        @pl.when(jnp.logical_not(fixed))
        def _():
            z_move().wait()

        gather_own(zs, az0, az1)
        start(gather_a(zs, az0, az1, AZA))
        wait(z_fourth())

    def hook4():
        wait(gather_a(zs, az0, az1, AZA))
        wait(gather_b(ax0, ax1, AXB))
        start(gather_b(az0, az1, AZB))

    def block_arrive(dst, base, at_y):
        @pl.when(y == at_y)
        def _():
            for cp in block_second(dst, base, at_y):
                cp.wait_send()

        @pl.when(y != at_y)
        def _():
            for d in range(3):
                @pl.when(lax.rem(at_y + d + 1, 4) == y)
                def _():
                    block_second(dst, base, at_y)[d].wait_recv()

        start(block_third(dst, base))

    def hook7():
        block_arrive(qc, QQ, 0)
        block_arrive(pc, PAN, pan_y)

    def hook8():
        wait(block_third(qc, QQ))
        wait(block_third(pc, PAN))
        wait(gather_b(az0, az1, AZB))

        @pl.when((y == pan_y) & (k == pan_k))
        def _():
            block_first(pan_src(1 - pan_k), pc, PAN, pan_y, pan_k).wait_send()

        @pl.when(r == 0)
        def _():
            block_first(trail_ref.at[pl.ds(256, 256)], qc, QQ, 0, 0).wait_send()

        @pl.when(c == 0)
        def _():
            for cp in first_cols_out():
                cp.wait_send()

    hooks = {0: hook0, 1: hook1, 2: hook2, 4: hook4, 7: hook7, 8: hook8}
    r_i = lax.broadcasted_iota(jnp.int32, (B, B), 0)
    c_i = lax.broadcasted_iota(jnp.int32, (B, B), 1)
    eye = (r_i == c_i).astype(jnp.float32)
    r_ref[...] = jnp.zeros_like(r_ref)
    rit_ref[...] = jnp.zeros_like(rit_ref)
    lui_ref[...] = jnp.zeros_like(lui_ref)
    mi_ref[...] = jnp.zeros_like(mi_ref)
    for t in range(3):
        e_ref[t, :, :B] = eye
        e_ref[t, :, B:] = eye

    def diag(v):
        return jnp.sum(jnp.where(r_i == c_i, v, 0.0), axis=1, keepdims=True)

    def pre(p):
        a, b = p * B, (p + 1) * B
        if p < NPH:
            block = x_ref[a:b, a:b]
            e_ref[0, :, :B] = jnp.where(r_i <= c_i, block, block.T)
            e_ref[0, :, B:] = eye
        if p > 0:
            a, b = a - B, b - B
            block = s_ref[a:b, a:b]
            e_ref[1, :, :B] = block
            e_ref[1, :, B:] = eye
            e_ref[2, :, :B] = block.T
            e_ref[2, :, B:] = eye

    def post(p):
        a, b = p * B, (p + 1) * B
        if p < NPH:
            left = e_ref[0, :, :B]
            rs = lax.rsqrt(diag(left))
            linv = rs * e_ref[0, :, B:]
            rpp = jnp.where(r_i <= c_i, rs * left, 0.0)
            r_ref[a:b, a:b] = rpp
            rit_ref[a:b, a:b] = linv
            if p:
                rit_ref[a:b, :a] = dot(linv, rit_ref[a:b, :a])
            s_ref[a:b, a:b] += rpp
            if b < NB:
                rrow = dot(linv, x_ref[a:b, b:])
                r_ref[a:b, b:] = rrow
                s_ref[a:b, b:] += rrow
                x_ref[b:, b:] -= dot_t(rrow, rrow)
                rit_ref[b:, :b] -= dot_t(rrow, rit_ref[a:b, :b])
        if p > 0:
            a, b = a - B, b - B
            lui = e_ref[1, :, B:]
            mit = (1.0 / diag(e_ref[2, :, :B])) * e_ref[2, :, B:]
            mi = mit.T
            lui_ref[a:b, a:b] = lui
            mi_ref[a:b, a:b] = mi
            if a:
                lui_ref[a:b, :a] = dot(lui, lui_ref[a:b, :a])
                mi_ref[:a, a:b] = dot(mi_ref[:a, a:b], mi)
            if b < NB:
                mrow = dot(lui, s_ref[a:b, b:])
                lucol = dot(s_ref[b:, a:b], mi)
                s_ref[b:, b:] -= dot(lucol, mrow)
                lui_ref[b:, :b] -= dot(lucol, lui_ref[a:b, :b])
                mi_ref[:b, b:] -= dot(mi_ref[:b, a:b], mrow)

    def phase(ph, carry):
        for p in range(NPH + 1):
            pl.when(ph == p)(functools.partial(pre, p))
        eliminate(e_ref, 3)
        for p in range(NPH + 1):
            pl.when(ph == p)(functools.partial(post, p))
        for p, hook in hooks.items():
            pl.when(ph == p)(hook)
        return carry

    lax.fori_loop(0, NPH + 1, phase, 0)


    k2t[...] = dot(lui_ref[...], rit_ref[...])
    k2 = split(k2t[...])
    lui = split(lui_ref[...])
    for az, ax, h in ((az0, ax0, 0), (az1, ax1, 1)):
        val = dot3(az[...].reshape(NB, NB), k2, NT) + dot3(ax[...].reshape(NB, NB), lui, NT)
        for n in range(16):
            j = 4 * (n % 4) + n // 4 if h == 0 else n
            img[64 * j + 32 * h : 64 * j + 32 * h + 32, :] = val[32 * n : 32 * n + 32, :]

    def shifted(q):
        block = panel_ref[256 * q : 256 * (q + 1), :]
        if q < 2:
            block = block + jnp.where(r == 0, r_ref[256 * q : 256 * (q + 1), :], 0.0)
        return block

    for q in range(4):
        wr[256 * q : 256 * (q + 1), :] = dot3(shifted(q), k2, NT)
    curv.fill(lambda i: dot3(wr[:, i * T : (i + 1) * T].T, img[:, i * T :]))
    start(curv.first())
    mi = split(mi_ref[...])
    for h in range(2):
        block = pc[h] + jnp.where(c == 0, r_ref[256 * h : 256 * (h + 1), :], 0.0)
        vc[256 * h : 256 * (h + 1), :] = dot3(block, mi)
    wait(curv.first())
    curv.add_pair()
    start(curv.second())
    for q in range(4):
        vec_ref[256 * q : 256 * (q + 1), :] = dot3(shifted(q), mi)
    wait(curv.second())
    curv.add_ring()
    start(curv.third())
    yct[...] = dot3(k2, zc[...].reshape(NB, NB), NT) + dot3(lui, qc[...].reshape(NB, NB))
    wait(curv.third())
    start(curv.fourth())
    vcs = split(vc[...])
    for q in range(4):
        rows = pl.ds(256 * q, 256)
        out_ref[rows, :] = trail_ref[rows, :] - dot3(img[rows, :], vcs, NT)
    wait(curv.fourth())

    def put_c(i, m, j, v):
        cc[i : i + m, j : j + T] = v
        if i // T * T != j:
            cc[j : j + T, i : i + m] = v.T

    curv.unpack(put_c)
    dct = split(yct[...] - dot3(cc[...], vcs, NT))
    for q in range(4):
        rows = pl.ds(256 * q, 256)
        out_ref[rows, :] -= dot3(vec_ref[rows, :], dct)


def on_device(panel, trailing):
    f32 = jnp.float32
    vm = pl.BlockSpec(memory_space=pltpu.VMEM)
    sq = pltpu.VMEM((NB, NB), f32)
    sums = [(8, PIECE, T), (4, PIECE, T), (4, PIECE, T), (3, PIECE, T), (8, PIECE, T)]
    shapes = [(NB, NB)] * 6 + [(3, B, 2 * B)] + sums * 2 + [
        (2, 16, 16, NB),
        (8, 64, NB), (4, 64, NB), (4, 64, NB), (3, 64, NB), (4, 2, 64, NB),
        (64, NB), (64, NB),
        (16, 32, NB), (16, 32, NB), (16, 32, NB), (16, 32, NB),
        (2, 256, NB), (2, 256, NB),
        (NB, NB), (1024, NB), (1024, NB), (NB, NB), (NB, NB), (NB, NB),
    ]
    return tuple(pl.pallas_call(
        step_kernel,
        out_shape=[jax.ShapeDtypeStruct((1024, NB), f32)] * 2,
        in_specs=[vm] * 2,
        out_specs=[vm] * 2,
        scratch_shapes=[pltpu.VMEM(s, f32) for s in shapes]
        + [pltpu.SemaphoreType.DMA((96,)), pltpu.SemaphoreType.DMA((72,))],
        compiler_params=pltpu.CompilerParams(
            vmem_limit_bytes=56 * 1024 * 1024, collective_id=0, has_side_effects=True),
        name="step",
    )(panel, trailing))


def solution(mesh):
    return jax.shard_map(
        on_device,
        mesh=mesh,
        in_specs=(P("row", None), P("row", "col")),
        out_specs=(P("row", "col"), P("row", None)),
        check_vma=False,
    )
```

```python
import functools
import jax, jax.numpy as jnp
from jax import lax
from jax.experimental import pallas as pl
from jax.experimental.pallas import tpu as pltpu
from jax.sharding import PartitionSpec as P

HI = lax.Precision.HIGHEST
MESH = pl.DeviceIdType.MESH
B = 64
NB = 512
NPH = NB // B
T = 128
PAIRS = [(i, j) for i in range(NB // T) for j in range(i, NB // T)]
PIECE = len(PAIRS) * T // 8


def dot(a, b):
    return lax.dot_general(a, b, (((1,), (0,)), ((), ())), precision=HI, preferred_element_type=jnp.float32)


def dot_t(a, b):
    return lax.dot_general(a, b, (((0,), (0,)), ((), ())), precision=HI, preferred_element_type=jnp.float32)


def split(a):
    hi = a.astype(jnp.bfloat16)
    return hi, (a - hi.astype(jnp.float32)).astype(jnp.bfloat16)


def dot3(a, b, dims=((1,), (0,))):
    (ah, al), (bh, bl) = (v if isinstance(v, tuple) else split(v) for v in (a, b))

    def one(p, q):
        return lax.dot_general(p, q, (dims, ((), ())), preferred_element_type=jnp.float32)

    return one(ah, bh) + (one(ah, bl) + one(al, bh))


NT = ((1,), (1,))
TN = ((0,), (0,))


def eliminate(e_ref, count):
    sub = lax.broadcasted_iota(jnp.int32, (8, 128), 0)
    rows = [[e_ref[t, 8 * i : 8 * i + 8, :] for i in range(B // 8)] for t in range(count)]

    def lane(v, k):
        return jnp.broadcast_to(v[:, k : k + 1], (8, 128))

    def row(v, k):
        return jnp.broadcast_to(v[k : k + 1, :], (8, 128))

    for jb in range(B // 8):
        full = [rows[t][jb] for t in range(count)]
        cols = [[lane(full[t], 8 * jb + m) for m in range(8)] for t in range(count)]
        kept = list(full)
        for m in range(8):
            for t in range(count):
                here = sub == m
                col = cols[t][m]
                rp = 1.0 / row(col, m)
                if m:
                    kept[t] = jnp.where(here, full[t], kept[t])
                scaled = row(full[t], m) * rp
                full[t] = jnp.where(here, scaled, full[t] - col * scaled)
                for k in range(m + 1, 8):
                    scaled = row(cols[t][k], m) * rp
                    cols[t][k] = jnp.where(here, scaled, cols[t][k] - col * scaled)
        for t in range(count):
            rows[t][jb] = kept[t]
            spread = [row(full[t], m) for m in range(8)]
            for i in range(jb + 1, B // 8):
                terms = [lane(rows[t][i], 8 * jb + m) * spread[m] for m in range(8)]
                while len(terms) > 1:
                    terms = [terms[k] + terms[k + 1] for k in range(0, len(terms), 2)]
                rows[t][i] = rows[t][i] - terms[0]
    for t in range(count):
        for i in range(B // 8):
            e_ref[t, 8 * i : 8 * i + 8, :] = rows[t][i]


def remote(src, dst, sends, recvs, n, device):
    return pltpu.make_async_remote_copy(
        src_ref=src, dst_ref=dst, send_sem=sends.at[n], recv_sem=recvs.at[n],
        device_id=device, device_id_type=MESH,
    )


class Sum:
    def __init__(self, bufs, sems, base, here):
        self.gp, self.other, self.half, self.parts, self.total = bufs
        self.sems, self.base, self.here = sems, base, here

    def fill(self, strip_of):
        for i in range(NB // T):
            strip = strip_of(i)
            for j in range(i, NB // T):
                n = PAIRS.index((i, j)) * T
                done = 0
                while done < T:
                    q, o = divmod(n + done, PIECE)
                    m = min(T - done, PIECE - o)
                    self.gp[q, o : o + m, :] = strip[done : done + m, (j - i) * T : (j - i + 1) * T]
                    done += m

    def first(self):
        k, mate = self.here["k"], self.here["mate"]
        return [remote(self.gp.at[pl.ds(4 * (1 - k), 4)], self.other, *self.sems, self.base, mate)]

    def add_pair(self):
        self.half[...] = self.gp[pl.ds(4 * self.here["k"], 4)] + self.other[...]

    def second(self):
        h = self.here
        return [
            remote(self.half.at[h["ys"][d]], self.parts.at[d], *self.sems, self.base + 1 + d, h["y_mates"][d])
            for d in range(3)
        ]

    def add_ring(self):
        k, y = self.here["k"], self.here["y"]
        self.total[4 * k + y] = (self.half[y] + self.parts[0]) + (self.parts[1] + self.parts[2])

    def third(self):
        h = self.here
        slot = self.total.at[4 * h["k"] + h["y"]]
        return [remote(slot, slot, *self.sems, self.base + 4 + d, h["y_mates"][d]) for d in range(3)]

    def fourth(self):
        group = self.total.at[pl.ds(4 * self.here["k"], 4)]
        return [remote(group, group, *self.sems, self.base + 7, self.here["mate"])]

    def unpack(self, store):
        for n, (i, j) in enumerate(PAIRS):
            done = 0
            while done < T:
                q, o = divmod(n * T + done, PIECE)
                m = min(T - done, PIECE - o)
                store(i * T + done, m, j * T, self.total[q, o : o + m, :])
                done += m


def start(copies):
    for cp in copies:
        cp.start()


def wait(copies):
    for cp in copies:
        cp.wait()


def step_kernel(
    panel_ref, trail_ref, out_ref, vec_ref,
    r_ref, rit_ref, lui_ref, mi_ref, x_ref, s_ref, e_ref,
    g0, g1, g2, g3, g4, c0, c1, c2, c3, c4,
    top, zp, zo, zh, zparts, zc, zs, xs, xt8, az0, az1, ax0, ax1, py, pc, qc,
    k2t, img, wr, vc, yct, cc, sends, recvs,
):
    r, c = lax.axis_index("row"), lax.axis_index("col")
    y, k = lax.div(r, 2), lax.rem(r, 2)
    x, z = lax.div(c, 4), lax.rem(c, 4)
    ys = [lax.rem(y + d, 4) for d in range(1, 4)]
    mate = (2 * y + 1 - k, c)
    y_mates = [(2 * v + k, c) for v in ys]
    y_cross = [(2 * v + 1 - k, c) for v in ys]
    x_mates = [(r, lax.rem(x + d, 4) * 4 + z) for d in range(1, 4)]
    z_mates = [(r, x * 4 + lax.rem(z + d, 4)) for d in range(1, 4)]
    peers = [mate] + y_mates + y_cross + x_mates + z_mates
    sems = (sends, recvs)
    here = {"k": k, "y": y, "ys": ys, "mate": mate, "y_mates": y_mates}
    to_r, to_c = lax.div(c, 2), 8 * lax.rem(c, 2) + r
    from_r, from_c = lax.rem(c, 8), 2 * r + lax.div(c, 8)
    fixed = (to_r == r) & (to_c == c)

    barrier = pltpu.get_barrier_semaphore()
    for peer in peers:
        pl.semaphore_signal(barrier, inc=1, device_id=peer, device_id_type=MESH)

    @pl.when(jnp.logical_not(fixed))
    def _():
        pl.semaphore_signal(barrier, inc=1, device_id=(from_r, from_c), device_id_type=MESH)

    lone = (r == 0) & (c == 0)

    @pl.when(jnp.logical_not(lone))
    def _():
        pl.semaphore_signal(barrier, inc=1, device_id=(0, 2 * r + lax.div(c, 8)), device_id_type=MESH)

    gram = Sum((g0, g1, g2, g3, g4), sems, 0, here)
    curv = Sum((c0, c1, c2, c3, c4), sems, 8, here)
    TOP, ZRS, ZAG, PERM, XSC, AXA, AXB, AZA, AZB, PAN, QQ = 16, 24, 28, 32, 33, 34, 40, 46, 52, 58, 66
    FAN = 72

    gram.fill(lambda i: dot_t(panel_ref[:, i * T : (i + 1) * T], panel_ref[:, i * T :]))

    pl.semaphore_wait(barrier, len(peers) + jnp.where(r == 0, 8, 0) - jnp.where(lone, 1, 0) + jnp.where(fixed, 0, 1))

    def top_out():
        out = []
        for n, peer in enumerate([(1, c)] + [(2 * v + q, c) for v in range(1, 4) for q in range(2)]):
            q = 1 if n == 0 else (n - 1) % 2
            place = x + 4 * z if q == 0 else z + 4 * x
            out.append(pltpu.make_async_remote_copy(
                src_ref=panel_ref.at[pl.ds(pl.multiple_of(32 * c + 16 * q, 16), 16)],
                dst_ref=top.at[q, place], send_sem=sends.at[FAN + n], recv_sem=recvs.at[TOP],
                device_id=peer, device_id_type=MESH))
        return out

    mine = jnp.where(k == 0, x + 4 * z, z + 4 * x)

    def top_spread(base, src, peers_0, peers_1):
        return [
            remote(src, src, sends, recvs, base + d, (r, jnp.where(k == 0, peers_0[d][1], peers_1[d][1])))
            for d in range(3)
        ]

    top_a = lambda: top_spread(TOP + 1, top.at[k, mine], x_mates, z_mates)
    top_b = lambda: top_spread(TOP + 4, top.at[k, pl.ds(4 * jnp.where(k == 0, z, x), 4)], z_mates, x_mates)
    top_c = lambda: [remote(top.at[k], top.at[k], sends, recvs, TOP + 7, mate)]

    def first_cols_out(n):
        return pltpu.make_async_remote_copy(
            src_ref=xt8.at[n], dst_ref=xs, send_sem=sends.at[FAN + 7 + n],
            recv_sem=recvs.at[XSC], device_id=(lax.div(c, 2), 8 * lax.rem(c, 2) + n), device_id_type=MESH)

    def first_cols(act):
        for n in range(1, 8):
            act(first_cols_out(n))

        @pl.when(c > 0)
        def _():
            act(first_cols_out(0))

    def gather_a(src, h0, h1, base):
        return [remote(src.at[pl.ds(0, 32)], h0.at[4 * z + x], sends, recvs, base + d, x_mates[d]) for d in range(3)] + [
            remote(src.at[pl.ds(32, 32)], h1.at[4 * x + z], sends, recvs, base + 3 + d, z_mates[d]) for d in range(3)]

    def gather_own(src, h0, h1):
        h0[4 * z + x] = src[0:32, :]
        h1[4 * x + z] = src[32:64, :]

    def gather_b(h0, h1, base):
        g0_, g1_ = h0.at[pl.ds(4 * z, 4)], h1.at[pl.ds(4 * x, 4)]
        return [remote(g0_, g0_, sends, recvs, base + d, z_mates[d]) for d in range(3)] + [
            remote(g1_, g1_, sends, recvs, base + 3 + d, x_mates[d]) for d in range(3)]

    def z_first():
        return [remote(zp.at[pl.ds(4 * (1 - k), 4)], zo, sends, recvs, ZRS, mate)]

    def z_second():
        return [remote(zh.at[ys[d]], zparts.at[d], sends, recvs, ZRS + 1 + d, y_mates[d]) for d in range(3)]

    def z_third():
        slot = zc.at[y, k]
        return [remote(slot, slot, sends, recvs, ZAG + d, y_mates[d]) for d in range(3)]

    def z_fourth():
        return [remote(zc.at[:, k], zc.at[:, k], sends, recvs, ZAG + 3, mate)]

    def z_move():
        return remote(zc.at[y, k], zs, sends, recvs, PERM, (to_r, to_c))

    def block_first(src_half, dst, base, at_y, at_k):
        return remote(src_half, dst.at[1 - at_k], sends, recvs, base, mate)

    def block_second(dst, base, at_y):
        return [remote(dst.at[k], dst.at[k], sends, recvs, base + 1 + d, y_mates[d]) for d in range(3)]

    def block_third(dst, base):
        return [remote(dst.at[k], dst.at[k], sends, recvs, base + 4, mate)]

    giver = k == lax.div(z, 2)
    given = 512 * lax.rem(z, 2)

    def pan_first():
        out = []
        for d in range(3):
            for q, peer in ((0, (2 * ys[d], c)), (1, (2 * ys[d] + 1, c))):
                out.append(pltpu.make_async_remote_copy(
                    src_ref=panel_ref.at[pl.ds(pl.multiple_of(given + 128 * x + 64 * q, 64), 64)],
                    dst_ref=py.at[d], send_sem=sends.at[FAN + 22 + 2 * d + q], recv_sem=recvs.at[PAN + d],
                    device_id=peer, device_id_type=MESH))
        return out

    def pan_first_arrived():
        for d in range(3):
            remote(py.at[d], py.at[d], sends, recvs, PAN + d, mate).wait_recv()

    def pan_second(act):
        for d in range(3):
            xt = lax.rem(x + d + 1, 4)

            @pl.when(xt != y)
            def _():
                act(remote(py.at[lax.rem(y - xt + 4, 4) - 1], pc.at[k, x], sends, recvs, PAN + 3 + d, (r, 4 * xt + z)))

    def pan_third(q, n):
        return remote(pc.at[q], pc.at[q], sends, recvs, PAN + 6 + n, mate)

    start(gram.first())
    pl.when(r == 0)(lambda: start(top_out()))

    @pl.when(r == 0)
    def _():
        for n in range(4):
            block = trail_ref[0:512, 128 * n : 128 * (n + 1)].T
            xt8[2 * n] = block[0:64, :]
            xt8[2 * n + 1] = block[64:128, :]
        first_cols(lambda cp: cp.start())
        block_first(trail_ref.at[pl.ds(256, 256)], qc, QQ, 0, 0).start()
        qc[0] = trail_ref[0:256, :]
        top[0, x + 4 * z] = panel_ref[pl.ds(pl.multiple_of(32 * c, 32), 16), :]

    @pl.when(lone)
    def _():
        xs[...] = xt8[0]

    wait(gram.first())
    gram.add_pair()
    start(gram.second())

    for half in range(2):
        acc = None
        for q in range(4):
            left = trail_ref[256 * q : 256 * (q + 1), 256 * half : 256 * (half + 1)].T
            term = dot3(left, panel_ref[256 * q : 256 * (q + 1), :])
            acc = term if acc is None else acc + term
        for q in range(4):
            s = 4 * half + q
            zp[4 * (s % 2) + s // 2] = acc[64 * q : 64 * (q + 1), :]
    start(z_first())

    @pl.when(r > 0)
    def _():
        remote(top.at[k, mine], top.at[k, mine], sends, recvs, TOP, mate).wait_recv()

    start(top_a())
    wait(gram.second())
    gram.add_ring()
    start(gram.third())
    wait(z_first())
    zh[...] = zp[pl.ds(4 * k, 4)] + zo[...]
    wait(top_a())
    start(top_b())
    wait(gram.third())
    start(gram.fourth())
    start(z_second())
    pl.when(giver)(lambda: start(pan_first()))
    wait(gram.fourth())

    def put(i, m, j, v):
        x_ref[i : i + m, j : j + T] = v

    gram.unpack(put)
    wait(top_b())
    start(top_c())

    @pl.when(jnp.logical_not(lone))
    def _():
        remote(xs, xs, sends, recvs, XSC, mate).wait_recv()

    gather_own(xs, ax0, ax1)
    start(gather_a(xs, ax0, ax1, AXA))

    def mid0():
        wait(z_second())
        zc[y, k] = (zh[y] + zparts[0]) + (zparts[1] + zparts[2])

        @pl.when(fixed)
        def _():
            zs[...] = zc[y, k]

        @pl.when(jnp.logical_not(fixed))
        def _():
            z_move().start()

        start(z_third())

    def hook0():
        wait(top_c())
        for a in range(4):
            for b in range(4):
                s_ref[32 * (4 * a + b) : 32 * (4 * a + b) + 16, :] += top[0, a + 4 * b]
                s_ref[32 * (4 * a + b) + 16 : 32 * (4 * a + b) + 32, :] += top[1, b + 4 * a]

    def mid1():
        wait(gather_a(xs, ax0, ax1, AXA))
        start(gather_b(ax0, ax1, AXB))

    def hook1():
        @pl.when(jnp.logical_not(fixed))
        def _():
            z_move().wait()

        gather_own(zs, az0, az1)
        start(gather_a(zs, az0, az1, AZA))

    def mid2():
        pan_first_arrived()
        pan_second(lambda cp: cp.start())

        @pl.when(x != y)
        def _():
            pc[k, x] = py[lax.rem(y - x + 4, 4) - 1]

        @pl.when((x == y) & giver)
        def _():
            for q in range(4):
                for h in range(2):
                    pc[h, q] = panel_ref[pl.ds(pl.multiple_of(given + 128 * q + 64 * h, 64), 64), :]
            pan_third(k, 0).start()
            pan_third(1 - k, 1).start()

        @pl.when(y == 0)
        def _():
            @pl.when(k != 0)
            def _():
                block_first(trail_ref.at[pl.ds(256, 256)], qc, QQ, 0, 0).wait_recv()

            start(block_second(qc, QQ, 0))

    def hook2():
        wait(z_third())
        start(z_fourth())

    def hook3():
        wait(gather_a(zs, az0, az1, AZA))
        start(gather_b(az0, az1, AZB))

    def hook4():
        @pl.when(x != y)
        def _():
            for d in range(3):
                remote(pc.at[k, 0], pc.at[k, 0], sends, recvs, PAN + 3 + d, mate).wait_recv()
            pan_third(k, 0).start()

    def block_arrive(dst, base, at_y):
        @pl.when(y == at_y)
        def _():
            for cp in block_second(dst, base, at_y):
                cp.wait_send()

        @pl.when(y != at_y)
        def _():
            for d in range(3):
                @pl.when(lax.rem(at_y + d + 1, 4) == y)
                def _():
                    block_second(dst, base, at_y)[d].wait_recv()

        start(block_third(dst, base))

    def hook6():
        wait(z_fourth())
        wait(gather_b(ax0, ax1, AXB))
        pan_second(lambda cp: cp.wait_send())

        @pl.when(x != y)
        def _():
            pan_third(k, 0).wait()

        @pl.when((x == y) & giver)
        def _():
            pan_third(k, 0).wait_send()
            pan_third(1 - k, 1).wait_send()

        @pl.when((x == y) & jnp.logical_not(giver))
        def _():
            pan_third(1 - k, 0).wait_recv()
            pan_third(k, 1).wait_recv()

    def hook7():
        block_arrive(qc, QQ, 0)

    def hook8():
        wait(block_third(qc, QQ))
        wait(gather_b(az0, az1, AZB))

        @pl.when(giver)
        def _():
            for cp in pan_first():
                cp.wait_send()

        @pl.when(r == 0)
        def _():
            for cp in top_out():
                cp.wait_send()
            first_cols(lambda cp: cp.wait_send())
            block_first(trail_ref.at[pl.ds(256, 256)], qc, QQ, 0, 0).wait_send()


    mids = {0: mid0, 1: mid1, 2: mid2}
    hooks = {0: hook0, 1: hook1, 2: hook2, 3: hook3, 4: hook4, 6: hook6, 7: hook7, 8: hook8}
    r_i = lax.broadcasted_iota(jnp.int32, (B, B), 0)
    c_i = lax.broadcasted_iota(jnp.int32, (B, B), 1)
    eye = (r_i == c_i).astype(jnp.float32)
    s_ref[...] = jnp.zeros_like(s_ref)
    r_ref[...] = jnp.zeros_like(r_ref)
    rit_ref[...] = jnp.zeros_like(rit_ref)
    lui_ref[...] = jnp.zeros_like(lui_ref)
    mi_ref[...] = jnp.zeros_like(mi_ref)
    for t in range(3):
        e_ref[t, :, :B] = eye
        e_ref[t, :, B:] = eye

    def diag(v):
        return jnp.sum(jnp.where(r_i == c_i, v, 0.0), axis=1, keepdims=True)

    def pre(p):
        a, b = p * B, (p + 1) * B
        if p < NPH:
            block = x_ref[a:b, a:b]
            e_ref[0, :, :B] = jnp.where(r_i <= c_i, block, block.T)
            e_ref[0, :, B:] = eye
        if p > 0:
            a, b = a - B, b - B
            block = s_ref[a:b, a:b]
            e_ref[1, :, :B] = block
            e_ref[1, :, B:] = eye
            e_ref[2, :, :B] = block.T
            e_ref[2, :, B:] = eye

    def post(p):
        a, b = p * B, (p + 1) * B
        if p < NPH:
            left = e_ref[0, :, :B]
            rs = lax.rsqrt(diag(left))
            linv = rs * e_ref[0, :, B:]
            rpp = jnp.where(r_i <= c_i, rs * left, 0.0)
            r_ref[a:b, a:b] = rpp
            rit_ref[a:b, a:b] = linv
            if p:
                rit_ref[a:b, :a] = dot(linv, rit_ref[a:b, :a])
            s_ref[a:b, a:b] += rpp
            if b < NB:
                rrow = dot(linv, x_ref[a:b, b:])
                r_ref[a:b, b:] = rrow
                s_ref[a:b, b:] += rrow
                x_ref[b:, b:] -= dot_t(rrow, rrow)
                rit_ref[b:, :b] -= dot_t(rrow, rit_ref[a:b, :b])
        if p > 0:
            a, b = a - B, b - B
            lui = e_ref[1, :, B:]
            mit = (1.0 / diag(e_ref[2, :, :B])) * e_ref[2, :, B:]
            mi = mit.T
            lui_ref[a:b, a:b] = lui
            mi_ref[a:b, a:b] = mi
            if a:
                lui_ref[a:b, :a] = dot(lui, lui_ref[a:b, :a])
                mi_ref[:a, a:b] = dot(mi_ref[:a, a:b], mi)
            if b < NB:
                mrow = dot(lui, s_ref[a:b, b:])
                lucol = dot(s_ref[b:, a:b], mi)
                s_ref[b:, b:] -= dot(lucol, mrow)
                lui_ref[b:, :b] -= dot(lucol, lui_ref[a:b, :b])
                mi_ref[:b, b:] -= dot(mi_ref[:b, a:b], mrow)

    def phase(ph, carry):
        for p in range(NPH + 1):
            pl.when(ph == p)(functools.partial(pre, p))
        eliminate(e_ref, 3)
        for p, hook in mids.items():
            pl.when(ph == p)(hook)
        for p in range(NPH + 1):
            pl.when(ph == p)(functools.partial(post, p))
        for p, hook in hooks.items():
            pl.when(ph == p)(hook)
        return carry

    lax.fori_loop(0, NPH + 1, phase, 0)


    k2t[...] = dot3(lui_ref[...], rit_ref[...])
    k2 = split(k2t[...])
    lui = split(lui_ref[...])
    for az, ax, h in ((az0, ax0, 0), (az1, ax1, 1)):
        val = dot3(az[...].reshape(NB, NB), k2, NT) + dot3(ax[...].reshape(NB, NB), lui, NT)
        for n in range(16):
            j = 4 * (n % 4) + n // 4 if h == 0 else n
            img[64 * j + 32 * h : 64 * j + 32 * h + 32, :] = val[32 * n : 32 * n + 32, :]

    def shifted(q):
        block = panel_ref[256 * q : 256 * (q + 1), :]
        if q < 2:
            block = block + jnp.where(r == 0, r_ref[256 * q : 256 * (q + 1), :], 0.0)
        return block

    for q in range(4):
        wr[256 * q : 256 * (q + 1), :] = dot3(shifted(q), k2, NT)
    curv.fill(lambda i: dot3(wr[:, i * T : (i + 1) * T].T, img[:, i * T :]))
    start(curv.first())
    mi = split(mi_ref[...])
    for q in range(4):
        for h in range(2):
            rows = pl.ds(128 * q + 64 * h, 64)
            vc[rows, :] = pc[h, q] + jnp.where(c == 0, r_ref[rows, :], 0.0)
    vc[...] = dot3(vc[...], mi)
    wait(curv.first())
    curv.add_pair()
    start(curv.second())
    for q in range(4):
        vec_ref[256 * q : 256 * (q + 1), :] = dot3(shifted(q), mi)
    wait(curv.second())
    curv.add_ring()
    start(curv.third())
    yct[...] = dot3(k2, zc[...].reshape(NB, NB), NT) + dot3(lui, qc[...].reshape(NB, NB))
    wait(curv.third())
    start(curv.fourth())
    vcs = split(vc[...])
    for q in range(4):
        rows = pl.ds(256 * q, 256)
        out_ref[rows, :] = trail_ref[rows, :] - dot3(img[rows, :], vcs, NT)
    wait(curv.fourth())

    def put_c(i, m, j, v):
        cc[i : i + m, j : j + T] = v
        if i // T * T != j:
            cc[j : j + T, i : i + m] = v.T

    curv.unpack(put_c)
    dct = split(yct[...] - dot3(cc[...], vcs, NT))
    for q in range(4):
        rows = pl.ds(256 * q, 256)
        out_ref[rows, :] -= dot3(vec_ref[rows, :], dct)


def on_device(panel, trailing):
    f32 = jnp.float32
    vm = pl.BlockSpec(memory_space=pltpu.VMEM)
    sq = pltpu.VMEM((NB, NB), f32)
    sums = [(8, PIECE, T), (4, PIECE, T), (4, PIECE, T), (3, PIECE, T), (8, PIECE, T)]
    shapes = [(NB, NB)] * 6 + [(3, B, 2 * B)] + sums * 2 + [
        (2, 16, 16, NB),
        (8, 64, NB), (4, 64, NB), (4, 64, NB), (3, 64, NB), (4, 2, 64, NB),
        (64, NB), (64, NB), (8, 64, NB),
        (16, 32, NB), (16, 32, NB), (16, 32, NB), (16, 32, NB),
        (3, 64, NB), (2, 4, 64, NB), (2, 256, NB),
        (NB, NB), (1024, NB), (1024, NB), (NB, NB), (NB, NB), (NB, NB),
    ]
    return tuple(pl.pallas_call(
        step_kernel,
        out_shape=[jax.ShapeDtypeStruct((1024, NB), f32)] * 2,
        in_specs=[vm] * 2,
        out_specs=[vm] * 2,
        scratch_shapes=[pltpu.VMEM(s, f32) for s in shapes]
        + [pltpu.SemaphoreType.DMA((104,)), pltpu.SemaphoreType.DMA((72,))],
        compiler_params=pltpu.CompilerParams(
            vmem_limit_bytes=56 * 1024 * 1024, collective_id=0, has_side_effects=True),
        name="step",
    )(panel, trailing))


def solution(mesh):
    return jax.shard_map(
        on_device,
        mesh=mesh,
        in_specs=(P("row", None), P("row", "col")),
        out_specs=(P("row", "col"), P("row", None)),
        check_vma=False,
    )
```

```python
import functools
import jax, jax.numpy as jnp
from jax import lax
from jax.experimental import pallas as pl
from jax.experimental.pallas import tpu as pltpu
from jax.sharding import PartitionSpec as P

HI = lax.Precision.HIGHEST
MESH = pl.DeviceIdType.MESH
B = 64
NB = 512
NPH = NB // B
T = 128
PAIRS = [(i, j) for i in range(NB // T) for j in range(i, NB // T)]
PIECE = len(PAIRS) * T // 8


def dot(a, b):
    return lax.dot_general(a, b, (((1,), (0,)), ((), ())), precision=HI, preferred_element_type=jnp.float32)


def dot_t(a, b):
    return lax.dot_general(a, b, (((0,), (0,)), ((), ())), precision=HI, preferred_element_type=jnp.float32)


def split(a):
    hi = a.astype(jnp.bfloat16)
    return hi, (a - hi.astype(jnp.float32)).astype(jnp.bfloat16)


def dot3(a, b, dims=((1,), (0,))):
    (ah, al), (bh, bl) = (v if isinstance(v, tuple) else split(v) for v in (a, b))

    def one(p, q):
        return lax.dot_general(p, q, (dims, ((), ())), preferred_element_type=jnp.float32)

    return one(ah, bh) + (one(ah, bl) + one(al, bh))


NT = ((1,), (1,))
TN = ((0,), (0,))


def eliminate(e_ref, count):
    sub = lax.broadcasted_iota(jnp.int32, (8, 128), 0)
    rows = [[e_ref[t, 8 * i : 8 * i + 8, :] for i in range(B // 8)] for t in range(count)]

    def lane(v, k):
        return jnp.broadcast_to(v[:, k : k + 1], (8, 128))

    def row(v, k):
        return jnp.broadcast_to(v[k : k + 1, :], (8, 128))

    for jb in range(B // 8):
        full = [rows[t][jb] for t in range(count)]
        cols = [[lane(full[t], 8 * jb + m) for m in range(8)] for t in range(count)]
        kept = list(full)
        for m in range(8):
            for t in range(count):
                here = sub == m
                col = cols[t][m]
                rp = 1.0 / row(col, m)
                if m:
                    kept[t] = jnp.where(here, full[t], kept[t])
                scaled = row(full[t], m) * rp
                full[t] = jnp.where(here, scaled, full[t] - col * scaled)
                for k in range(m + 1, 8):
                    scaled = row(cols[t][k], m) * rp
                    cols[t][k] = jnp.where(here, scaled, cols[t][k] - col * scaled)
        for t in range(count):
            rows[t][jb] = kept[t]
            spread = [row(full[t], m) for m in range(8)]
            for i in range(jb + 1, B // 8):
                terms = [lane(rows[t][i], 8 * jb + m) * spread[m] for m in range(8)]
                while len(terms) > 1:
                    terms = [terms[k] + terms[k + 1] for k in range(0, len(terms), 2)]
                rows[t][i] = rows[t][i] - terms[0]
    for t in range(count):
        for i in range(B // 8):
            e_ref[t, 8 * i : 8 * i + 8, :] = rows[t][i]


def remote(src, dst, sends, recvs, n, device):
    return pltpu.make_async_remote_copy(
        src_ref=src, dst_ref=dst, send_sem=sends.at[n], recv_sem=recvs.at[n],
        device_id=device, device_id_type=MESH,
    )


class Sum:
    def __init__(self, bufs, sems, base, here):
        self.gp, self.other, self.half, self.parts, self.total = bufs
        self.sems, self.base, self.here = sems, base, here

    def fill(self, strip_of):
        for i in range(NB // T):
            strip = strip_of(i)
            for j in range(i, NB // T):
                n = PAIRS.index((i, j)) * T
                done = 0
                while done < T:
                    q, o = divmod(n + done, PIECE)
                    m = min(T - done, PIECE - o)
                    self.gp[q, o : o + m, :] = strip[done : done + m, (j - i) * T : (j - i + 1) * T]
                    done += m

    def first(self):
        k, mate = self.here["k"], self.here["mate"]
        return [remote(self.gp.at[pl.ds(4 * (1 - k), 4)], self.other, *self.sems, self.base, mate)]

    def add_pair(self):
        self.half[...] = self.gp[pl.ds(4 * self.here["k"], 4)] + self.other[...]

    def second(self):
        h = self.here
        return [
            remote(self.half.at[h["ys"][d]], self.parts.at[d], *self.sems, self.base + 1 + d, h["y_mates"][d])
            for d in range(3)
        ]

    def add_ring(self):
        k, y = self.here["k"], self.here["y"]
        self.total[4 * k + y] = (self.half[y] + self.parts[0]) + (self.parts[1] + self.parts[2])

    def third(self):
        h = self.here
        slot = self.total.at[4 * h["k"] + h["y"]]
        return [remote(slot, slot, *self.sems, self.base + 4 + d, h["y_mates"][d]) for d in range(3)]

    def fourth(self):
        group = self.total.at[pl.ds(4 * self.here["k"], 4)]
        return [remote(group, group, *self.sems, self.base + 7, self.here["mate"])]

    def unpack(self, store):
        for n, (i, j) in enumerate(PAIRS):
            done = 0
            while done < T:
                q, o = divmod(n * T + done, PIECE)
                m = min(T - done, PIECE - o)
                store(i * T + done, m, j * T, self.total[q, o : o + m, :])
                done += m


def start(copies):
    for cp in copies:
        cp.start()


def wait(copies):
    for cp in copies:
        cp.wait()


def step_kernel(
    panel_ref, trail_ref, out_ref, vec_ref,
    r_ref, rit_ref, lui_ref, mi_ref, x_ref, s_ref, e_ref,
    g0, g1, g2, g3, g4, c0, c1, c2, c3, c4,
    top, zp, zo, zh, zparts, zc, zs, xs, sx0, sx1, rx0, rx1, az0, az1, ax0, ax1, py, pc, qc,
    k2t, img, wr, vc, yct, cc, sends, recvs,
):
    r, c = lax.axis_index("row"), lax.axis_index("col")
    y, k = lax.div(r, 2), lax.rem(r, 2)
    x, z = lax.div(c, 4), lax.rem(c, 4)
    ys = [lax.rem(y + d, 4) for d in range(1, 4)]
    mate = (2 * y + 1 - k, c)
    y_mates = [(2 * v + k, c) for v in ys]
    y_cross = [(2 * v + 1 - k, c) for v in ys]
    x_mates = [(r, lax.rem(x + d, 4) * 4 + z) for d in range(1, 4)]
    z_mates = [(r, x * 4 + lax.rem(z + d, 4)) for d in range(1, 4)]
    peers = [mate] + y_mates + y_cross + x_mates + z_mates
    sems = (sends, recvs)
    here = {"k": k, "y": y, "ys": ys, "mate": mate, "y_mates": y_mates}
    to_r, to_c = lax.div(c, 2), 8 * lax.rem(c, 2) + r
    from_r, from_c = lax.rem(c, 8), 2 * r + lax.div(c, 8)
    fixed = (to_r == r) & (to_c == c)

    barrier = pltpu.get_barrier_semaphore()
    for peer in peers:
        pl.semaphore_signal(barrier, inc=1, device_id=peer, device_id_type=MESH)

    @pl.when(jnp.logical_not(fixed))
    def _():
        pl.semaphore_signal(barrier, inc=1, device_id=(from_r, from_c), device_id_type=MESH)


    gram = Sum((g0, g1, g2, g3, g4), sems, 0, here)
    curv = Sum((c0, c1, c2, c3, c4), sems, 8, here)
    TOP, ZRS, ZAG, PERM, XSC, AXA, AXB, AZA, AZB, PAN, QQ = 16, 24, 28, 32, 33, 37, 43, 49, 55, 61, 69
    FAN = 76

    gram.fill(lambda i: dot_t(panel_ref[:, i * T : (i + 1) * T], panel_ref[:, i * T :]))

    pl.semaphore_wait(barrier, len(peers) + jnp.where(fixed, 0, 1))

    def top_out():
        out = []
        for n, peer in enumerate([(1, c)] + [(2 * v + q, c) for v in range(1, 4) for q in range(2)]):
            q = 1 if n == 0 else (n - 1) % 2
            place = x + 4 * z if q == 0 else z + 4 * x
            out.append(pltpu.make_async_remote_copy(
                src_ref=panel_ref.at[pl.ds(pl.multiple_of(32 * c + 16 * q, 16), 16)],
                dst_ref=top.at[q, place], send_sem=sends.at[FAN + n], recv_sem=recvs.at[TOP],
                device_id=peer, device_id_type=MESH))
        return out

    mine = jnp.where(k == 0, x + 4 * z, z + 4 * x)

    def top_spread(base, src, peers_0, peers_1):
        return [
            remote(src, src, sends, recvs, base + d, (r, jnp.where(k == 0, peers_0[d][1], peers_1[d][1])))
            for d in range(3)
        ]

    top_a = lambda: top_spread(TOP + 1, top.at[k, mine], x_mates, z_mates)
    top_b = lambda: top_spread(TOP + 4, top.at[k, pl.ds(4 * jnp.where(k == 0, z, x), 4)], z_mates, x_mates)
    top_c = lambda: [remote(top.at[k], top.at[k], sends, recvs, TOP + 7, mate)]

    def scatter_first():
        out = []
        for d in range(3):
            out.append(pltpu.make_async_remote_copy(
                src_ref=sx0.at[d + 1], dst_ref=rx0, send_sem=sends.at[FAN + 7 + d], recv_sem=recvs.at[XSC],
                device_id=(r, d + 1), device_id_type=MESH))
            out.append(pltpu.make_async_remote_copy(
                src_ref=sx1.at[d + 1], dst_ref=rx1, send_sem=sends.at[FAN + 10 + d], recv_sem=recvs.at[XSC + 1],
                device_id=(r, 4 * (d + 1)), device_id_type=MESH))
        return out

    def scatter_second(axis):
        out = []
        for d in range(3):
            src, dst, to = (rx0, 0, 4 * (d + 1) + z) if axis == 0 else (rx1, 32, 4 * x + d + 1)
            out.append(pltpu.make_async_remote_copy(
                src_ref=src.at[d + 1], dst_ref=xs.at[pl.ds(dst, 32)], send_sem=sends.at[FAN + 13 + 3 * axis + d],
                recv_sem=recvs.at[XSC + 2 + axis], device_id=(r, to), device_id_type=MESH))
        return out

    def scatter_relay():
        @pl.when((x == 0) & (z > 0))
        def _():
            remote(rx0, rx0, sends, recvs, XSC, mate).wait_recv()

        @pl.when((z == 0) & (x > 0))
        def _():
            remote(rx1, rx1, sends, recvs, XSC + 1, mate).wait_recv()

        @pl.when(x == 0)
        def _():
            start(scatter_second(0))
            xs[0:32, :] = rx0[0]

        @pl.when(z == 0)
        def _():
            start(scatter_second(1))
            xs[32:64, :] = rx1[0]

    def scatter_arrived():
        @pl.when(x > 0)
        def _():
            remote(rx0.at[0], rx0.at[0], sends, recvs, XSC + 2, mate).wait_recv()

        @pl.when(z > 0)
        def _():
            remote(rx1.at[0], rx1.at[0], sends, recvs, XSC + 3, mate).wait_recv()

    def gather_a(src, h0, h1, base):
        return [remote(src.at[pl.ds(0, 32)], h0.at[4 * z + x], sends, recvs, base + d, x_mates[d]) for d in range(3)] + [
            remote(src.at[pl.ds(32, 32)], h1.at[4 * x + z], sends, recvs, base + 3 + d, z_mates[d]) for d in range(3)]

    def gather_own(src, h0, h1):
        h0[4 * z + x] = src[0:32, :]
        h1[4 * x + z] = src[32:64, :]

    def gather_b(h0, h1, base):
        g0_, g1_ = h0.at[pl.ds(4 * z, 4)], h1.at[pl.ds(4 * x, 4)]
        return [remote(g0_, g0_, sends, recvs, base + d, z_mates[d]) for d in range(3)] + [
            remote(g1_, g1_, sends, recvs, base + 3 + d, x_mates[d]) for d in range(3)]

    def z_first():
        return [remote(zp.at[pl.ds(4 * (1 - k), 4)], zo, sends, recvs, ZRS, mate)]

    def z_second():
        return [remote(zh.at[ys[d]], zparts.at[d], sends, recvs, ZRS + 1 + d, y_mates[d]) for d in range(3)]

    def z_third():
        slot = zc.at[y, k]
        return [remote(slot, slot, sends, recvs, ZAG + d, y_mates[d]) for d in range(3)]

    def z_fourth():
        return [remote(zc.at[:, k], zc.at[:, k], sends, recvs, ZAG + 3, mate)]

    def z_move():
        return remote(zc.at[y, k], zs, sends, recvs, PERM, (to_r, to_c))

    def block_first(src_half, dst, base, at_y, at_k):
        return remote(src_half, dst.at[1 - at_k], sends, recvs, base, mate)

    def block_second(dst, base, at_y):
        return [remote(dst.at[k], dst.at[k], sends, recvs, base + 1 + d, y_mates[d]) for d in range(3)]

    def block_third(dst, base):
        return [remote(dst.at[k], dst.at[k], sends, recvs, base + 4, mate)]

    giver = k == lax.div(z, 2)
    given = 512 * lax.rem(z, 2)

    def pan_first():
        out = []
        for d in range(3):
            for q, peer in ((0, (2 * ys[d], c)), (1, (2 * ys[d] + 1, c))):
                out.append(pltpu.make_async_remote_copy(
                    src_ref=panel_ref.at[pl.ds(pl.multiple_of(given + 128 * x + 64 * q, 64), 64)],
                    dst_ref=py.at[d], send_sem=sends.at[FAN + 22 + 2 * d + q], recv_sem=recvs.at[PAN + d],
                    device_id=peer, device_id_type=MESH))
        return out

    def pan_first_arrived():
        for d in range(3):
            remote(py.at[d], py.at[d], sends, recvs, PAN + d, mate).wait_recv()

    def pan_second(act):
        for d in range(3):
            xt = lax.rem(x + d + 1, 4)

            @pl.when(xt != y)
            def _():
                act(remote(py.at[lax.rem(y - xt + 4, 4) - 1], pc.at[k, x], sends, recvs, PAN + 3 + d, (r, 4 * xt + z)))

    def pan_third(q, n):
        return remote(pc.at[q], pc.at[q], sends, recvs, PAN + 6 + n, mate)

    start(gram.first())
    pl.when(r == 0)(lambda: start(top_out()))

    @pl.when(r == 0)
    def _():
        block_first(trail_ref.at[pl.ds(256, 256)], qc, QQ, 0, 0).start()
        qc[0] = trail_ref[0:256, :]
        top[0, x + 4 * z] = panel_ref[pl.ds(pl.multiple_of(32 * c, 32), 16), :]

    @pl.when(c == 0)
    def _():
        for n in range(16):
            sx0[n % 4, n // 4] = trail_ref[64 * n : 64 * n + 32, :]
            sx1[n // 4, n % 4] = trail_ref[64 * n + 32 : 64 * n + 64, :]
        start(scatter_first())
        rx0[...] = sx0[0]
        rx1[...] = sx1[0]

    wait(gram.first())
    gram.add_pair()
    start(gram.second())

    for half in range(2):
        acc = None
        for q in range(4):
            left = trail_ref[256 * q : 256 * (q + 1), 256 * half : 256 * (half + 1)].T
            term = dot3(left, panel_ref[256 * q : 256 * (q + 1), :])
            acc = term if acc is None else acc + term
        for q in range(4):
            s = 4 * half + q
            zp[4 * (s % 2) + s // 2] = acc[64 * q : 64 * (q + 1), :]
    start(z_first())

    @pl.when(r > 0)
    def _():
        remote(top.at[k, mine], top.at[k, mine], sends, recvs, TOP, mate).wait_recv()

    start(top_a())
    wait(gram.second())
    gram.add_ring()
    start(gram.third())
    wait(z_first())
    zh[...] = zp[pl.ds(4 * k, 4)] + zo[...]
    wait(top_a())
    start(top_b())
    scatter_relay()
    wait(gram.third())
    start(gram.fourth())
    start(z_second())
    pl.when(giver)(lambda: start(pan_first()))
    wait(gram.fourth())

    def put(i, m, j, v):
        x_ref[i : i + m, j : j + T] = v

    gram.unpack(put)
    wait(top_b())
    start(top_c())

    scatter_arrived()
    gather_own(xs, ax0, ax1)
    start(gather_a(xs, ax0, ax1, AXA))

    def mid0():
        wait(z_second())
        zc[y, k] = (zh[y] + zparts[0]) + (zparts[1] + zparts[2])

        @pl.when(fixed)
        def _():
            zs[...] = zc[y, k]

        @pl.when(jnp.logical_not(fixed))
        def _():
            z_move().start()

        start(z_third())

    def hook0():
        wait(top_c())
        for a in range(4):
            for b in range(4):
                s_ref[32 * (4 * a + b) : 32 * (4 * a + b) + 16, :] += top[0, a + 4 * b]
                s_ref[32 * (4 * a + b) + 16 : 32 * (4 * a + b) + 32, :] += top[1, b + 4 * a]

    def mid1():
        wait(gather_a(xs, ax0, ax1, AXA))
        start(gather_b(ax0, ax1, AXB))

    def hook1():
        @pl.when(jnp.logical_not(fixed))
        def _():
            z_move().wait()

        gather_own(zs, az0, az1)
        start(gather_a(zs, az0, az1, AZA))

    def mid2():
        pan_first_arrived()
        pan_second(lambda cp: cp.start())

        @pl.when(x != y)
        def _():
            pc[k, x] = py[lax.rem(y - x + 4, 4) - 1]

        @pl.when((x == y) & giver)
        def _():
            for q in range(4):
                for h in range(2):
                    pc[h, q] = panel_ref[pl.ds(pl.multiple_of(given + 128 * q + 64 * h, 64), 64), :]
            pan_third(k, 0).start()
            pan_third(1 - k, 1).start()

        @pl.when(y == 0)
        def _():
            @pl.when(k != 0)
            def _():
                block_first(trail_ref.at[pl.ds(256, 256)], qc, QQ, 0, 0).wait_recv()

            start(block_second(qc, QQ, 0))

    def hook2():
        wait(z_third())
        start(z_fourth())

    def hook3():
        wait(gather_a(zs, az0, az1, AZA))
        start(gather_b(az0, az1, AZB))

    def hook4():
        @pl.when(x != y)
        def _():
            for d in range(3):
                remote(pc.at[k, 0], pc.at[k, 0], sends, recvs, PAN + 3 + d, mate).wait_recv()
            pan_third(k, 0).start()

    def block_arrive(dst, base, at_y):
        @pl.when(y == at_y)
        def _():
            for cp in block_second(dst, base, at_y):
                cp.wait_send()

        @pl.when(y != at_y)
        def _():
            for d in range(3):
                @pl.when(lax.rem(at_y + d + 1, 4) == y)
                def _():
                    block_second(dst, base, at_y)[d].wait_recv()

        start(block_third(dst, base))

    def hook6():
        wait(z_fourth())
        wait(gather_b(ax0, ax1, AXB))
        pan_second(lambda cp: cp.wait_send())

        @pl.when(x != y)
        def _():
            pan_third(k, 0).wait()

        @pl.when((x == y) & giver)
        def _():
            pan_third(k, 0).wait_send()
            pan_third(1 - k, 1).wait_send()

        @pl.when((x == y) & jnp.logical_not(giver))
        def _():
            pan_third(1 - k, 0).wait_recv()
            pan_third(k, 1).wait_recv()

    def hook7():
        block_arrive(qc, QQ, 0)

    def hook8():
        wait(block_third(qc, QQ))
        wait(gather_b(az0, az1, AZB))

        @pl.when(giver)
        def _():
            for cp in pan_first():
                cp.wait_send()

        @pl.when(r == 0)
        def _():
            for cp in top_out():
                cp.wait_send()
            block_first(trail_ref.at[pl.ds(256, 256)], qc, QQ, 0, 0).wait_send()

        @pl.when(c == 0)
        def _():
            for cp in scatter_first():
                cp.wait_send()

        @pl.when(x == 0)
        def _():
            for cp in scatter_second(0):
                cp.wait_send()

        @pl.when(z == 0)
        def _():
            for cp in scatter_second(1):
                cp.wait_send()


    mids = {0: mid0, 1: mid1, 2: mid2}
    hooks = {0: hook0, 1: hook1, 2: hook2, 3: hook3, 4: hook4, 6: hook6, 7: hook7, 8: hook8}
    r_i = lax.broadcasted_iota(jnp.int32, (B, B), 0)
    c_i = lax.broadcasted_iota(jnp.int32, (B, B), 1)
    eye = (r_i == c_i).astype(jnp.float32)
    s_ref[...] = jnp.zeros_like(s_ref)
    r_ref[...] = jnp.zeros_like(r_ref)
    rit_ref[...] = jnp.zeros_like(rit_ref)
    lui_ref[...] = jnp.zeros_like(lui_ref)
    mi_ref[...] = jnp.zeros_like(mi_ref)
    for t in range(3):
        e_ref[t, :, :B] = eye
        e_ref[t, :, B:] = eye

    def diag(v):
        return jnp.sum(jnp.where(r_i == c_i, v, 0.0), axis=1, keepdims=True)

    def pre(p):
        a, b = p * B, (p + 1) * B
        if p < NPH:
            block = x_ref[a:b, a:b]
            e_ref[0, :, :B] = jnp.where(r_i <= c_i, block, block.T)
            e_ref[0, :, B:] = eye
        if p > 0:
            a, b = a - B, b - B
            block = s_ref[a:b, a:b]
            e_ref[1, :, :B] = block
            e_ref[1, :, B:] = eye
            e_ref[2, :, :B] = block.T
            e_ref[2, :, B:] = eye

    def post(p):
        a, b = p * B, (p + 1) * B
        if p < NPH:
            left = e_ref[0, :, :B]
            rs = lax.rsqrt(diag(left))
            linv = rs * e_ref[0, :, B:]
            rpp = jnp.where(r_i <= c_i, rs * left, 0.0)
            r_ref[a:b, a:b] = rpp
            rit_ref[a:b, a:b] = linv
            if p:
                rit_ref[a:b, :a] = dot(linv, rit_ref[a:b, :a])
            s_ref[a:b, a:b] += rpp
            if b < NB:
                rrow = dot(linv, x_ref[a:b, b:])
                r_ref[a:b, b:] = rrow
                s_ref[a:b, b:] += rrow
                x_ref[b:, b:] -= dot_t(rrow, rrow)
                rit_ref[b:, :b] -= dot_t(rrow, rit_ref[a:b, :b])
        if p > 0:
            a, b = a - B, b - B
            lui = e_ref[1, :, B:]
            mit = (1.0 / diag(e_ref[2, :, :B])) * e_ref[2, :, B:]
            mi = mit.T
            lui_ref[a:b, a:b] = lui
            mi_ref[a:b, a:b] = mi
            if a:
                lui_ref[a:b, :a] = dot(lui, lui_ref[a:b, :a])
                mi_ref[:a, a:b] = dot(mi_ref[:a, a:b], mi)
            if b < NB:
                mrow = dot(lui, s_ref[a:b, b:])
                lucol = dot(s_ref[b:, a:b], mi)
                s_ref[b:, b:] -= dot(lucol, mrow)
                lui_ref[b:, :b] -= dot(lucol, lui_ref[a:b, :b])
                mi_ref[:b, b:] -= dot(mi_ref[:b, a:b], mrow)

    def phase(ph, carry):
        for p in range(NPH + 1):
            pl.when(ph == p)(functools.partial(pre, p))
        eliminate(e_ref, 3)
        for p, hook in mids.items():
            pl.when(ph == p)(hook)
        for p in range(NPH + 1):
            pl.when(ph == p)(functools.partial(post, p))
        for p, hook in hooks.items():
            pl.when(ph == p)(hook)
        return carry

    lax.fori_loop(0, NPH + 1, phase, 0)


    k2t[...] = dot3(lui_ref[...], rit_ref[...])
    k2 = split(k2t[...])
    lui = split(lui_ref[...])
    for az, ax, h in ((az0, ax0, 0), (az1, ax1, 1)):
        val = dot3(az[...].reshape(NB, NB), k2, NT) + dot3(ax[...].reshape(NB, NB), lui, NT)
        for n in range(16):
            j = 4 * (n % 4) + n // 4 if h == 0 else n
            img[64 * j + 32 * h : 64 * j + 32 * h + 32, :] = val[32 * n : 32 * n + 32, :]

    def shifted(q):
        block = panel_ref[256 * q : 256 * (q + 1), :]
        if q < 2:
            block = block + jnp.where(r == 0, r_ref[256 * q : 256 * (q + 1), :], 0.0)
        return block

    for q in range(4):
        wr[256 * q : 256 * (q + 1), :] = dot3(shifted(q), k2, NT)
    curv.fill(lambda i: dot3(wr[:, i * T : (i + 1) * T].T, img[:, i * T :]))
    start(curv.first())
    mi = split(mi_ref[...])
    for q in range(4):
        for h in range(2):
            rows = pl.ds(128 * q + 64 * h, 64)
            vc[rows, :] = pc[h, q] + jnp.where(c == 0, r_ref[rows, :], 0.0)
    vc[...] = dot3(vc[...], mi)
    wait(curv.first())
    curv.add_pair()
    start(curv.second())
    for q in range(4):
        vec_ref[256 * q : 256 * (q + 1), :] = dot3(shifted(q), mi)
    wait(curv.second())
    curv.add_ring()
    start(curv.third())
    yct[...] = dot3(k2, zc[...].reshape(NB, NB), NT) + dot3(lui, qc[...].reshape(NB, NB))
    wait(curv.third())
    start(curv.fourth())
    vcs = split(vc[...])
    for q in range(4):
        rows = pl.ds(256 * q, 256)
        out_ref[rows, :] = trail_ref[rows, :] - dot3(img[rows, :], vcs, NT)
    wait(curv.fourth())

    def put_c(i, m, j, v):
        cc[i : i + m, j : j + T] = v
        if i // T * T != j:
            cc[j : j + T, i : i + m] = v.T

    curv.unpack(put_c)
    dct = split(yct[...] - dot3(cc[...], vcs, NT))
    for q in range(4):
        rows = pl.ds(256 * q, 256)
        out_ref[rows, :] -= dot3(vec_ref[rows, :], dct)


def on_device(panel, trailing):
    f32 = jnp.float32
    vm = pl.BlockSpec(memory_space=pltpu.VMEM)
    sq = pltpu.VMEM((NB, NB), f32)
    sums = [(8, PIECE, T), (4, PIECE, T), (4, PIECE, T), (3, PIECE, T), (8, PIECE, T)]
    shapes = [(NB, NB)] * 6 + [(3, B, 2 * B)] + sums * 2 + [
        (2, 16, 16, NB),
        (8, 64, NB), (4, 64, NB), (4, 64, NB), (3, 64, NB), (4, 2, 64, NB),
        (64, NB), (64, NB), (4, 4, 32, NB), (4, 4, 32, NB), (4, 32, NB), (4, 32, NB),
        (16, 32, NB), (16, 32, NB), (16, 32, NB), (16, 32, NB),
        (3, 64, NB), (2, 4, 64, NB), (2, 256, NB),
        (NB, NB), (1024, NB), (1024, NB), (NB, NB), (NB, NB), (NB, NB),
    ]
    return tuple(pl.pallas_call(
        step_kernel,
        out_shape=[jax.ShapeDtypeStruct((1024, NB), f32)] * 2,
        in_specs=[vm] * 2,
        out_specs=[vm] * 2,
        scratch_shapes=[pltpu.VMEM(s, f32) for s in shapes]
        + [pltpu.SemaphoreType.DMA((108,)), pltpu.SemaphoreType.DMA((76,))],
        compiler_params=pltpu.CompilerParams(
            vmem_limit_bytes=56 * 1024 * 1024, collective_id=0, has_side_effects=True),
        name="step",
    )(panel, trailing))


def solution(mesh):
    return jax.shard_map(
        on_device,
        mesh=mesh,
        in_specs=(P("row", None), P("row", "col")),
        out_specs=(P("row", "col"), P("row", None)),
        check_vma=False,
    )
```

```python
import functools
import jax, jax.numpy as jnp
from jax import lax
from jax.experimental import pallas as pl
from jax.experimental.pallas import tpu as pltpu
from jax.sharding import PartitionSpec as P

HI = lax.Precision.HIGHEST
MESH = pl.DeviceIdType.MESH
B = 64
NB = 512
NPH = NB // B
T = 128
PAIRS = [(i, j) for i in range(NB // T) for j in range(i, NB // T)]
PIECE = len(PAIRS) * T // 8


def dot(a, b):
    return lax.dot_general(a, b, (((1,), (0,)), ((), ())), precision=HI, preferred_element_type=jnp.float32)


def dot_t(a, b):
    return lax.dot_general(a, b, (((0,), (0,)), ((), ())), precision=HI, preferred_element_type=jnp.float32)


def split(a):
    hi = a.astype(jnp.bfloat16)
    return hi, (a - hi.astype(jnp.float32)).astype(jnp.bfloat16)


def dot3(a, b, dims=((1,), (0,))):
    (ah, al), (bh, bl) = (v if isinstance(v, tuple) else split(v) for v in (a, b))

    def one(p, q):
        return lax.dot_general(p, q, (dims, ((), ())), preferred_element_type=jnp.float32)

    return one(ah, bh) + (one(ah, bl) + one(al, bh))


NT = ((1,), (1,))
TN = ((0,), (0,))


def eliminate(e_ref, count):
    sub = lax.broadcasted_iota(jnp.int32, (8, 128), 0)
    rows = [[e_ref[t, 8 * i : 8 * i + 8, :] for i in range(B // 8)] for t in range(count)]

    def lane(v, k):
        return jnp.broadcast_to(v[:, k : k + 1], (8, 128))

    def row(v, k):
        return jnp.broadcast_to(v[k : k + 1, :], (8, 128))

    for jb in range(B // 8):
        full = [rows[t][jb] for t in range(count)]
        cols = [[lane(full[t], 8 * jb + m) for m in range(8)] for t in range(count)]
        kept = list(full)
        for m in range(8):
            for t in range(count):
                here = sub == m
                col = cols[t][m]
                rp = 1.0 / row(col, m)
                if m:
                    kept[t] = jnp.where(here, full[t], kept[t])
                scaled = row(full[t], m) * rp
                full[t] = jnp.where(here, scaled, full[t] - col * scaled)
                for k in range(m + 1, 8):
                    scaled = row(cols[t][k], m) * rp
                    cols[t][k] = jnp.where(here, scaled, cols[t][k] - col * scaled)
        for t in range(count):
            rows[t][jb] = kept[t]
            spread = [row(full[t], m) for m in range(8)]
            for i in range(jb + 1, B // 8):
                terms = [lane(rows[t][i], 8 * jb + m) * spread[m] for m in range(8)]
                while len(terms) > 1:
                    terms = [terms[k] + terms[k + 1] for k in range(0, len(terms), 2)]
                rows[t][i] = rows[t][i] - terms[0]
    for t in range(count):
        for i in range(B // 8):
            e_ref[t, 8 * i : 8 * i + 8, :] = rows[t][i]


def remote(src, dst, sends, recvs, n, device):
    return pltpu.make_async_remote_copy(
        src_ref=src, dst_ref=dst, send_sem=sends.at[n], recv_sem=recvs.at[n],
        device_id=device, device_id_type=MESH,
    )


class Sum:
    def __init__(self, bufs, sems, base, here):
        self.gp, self.other, self.half, self.parts, self.total = bufs
        self.sems, self.base, self.here = sems, base, here

    def fill(self, strip_of):
        for i in range(NB // T):
            strip = strip_of(i)
            for j in range(i, NB // T):
                n = PAIRS.index((i, j)) * T
                done = 0
                while done < T:
                    q, o = divmod(n + done, PIECE)
                    m = min(T - done, PIECE - o)
                    self.gp[q, o : o + m, :] = strip[done : done + m, (j - i) * T : (j - i + 1) * T]
                    done += m

    def first(self):
        k, mate = self.here["k"], self.here["mate"]
        return [remote(self.gp.at[pl.ds(4 * (1 - k), 4)], self.other, *self.sems, self.base, mate)]

    def add_pair(self):
        self.half[...] = self.gp[pl.ds(4 * self.here["k"], 4)] + self.other[...]

    def second(self):
        h = self.here
        return [
            remote(self.half.at[h["ys"][d]], self.parts.at[d], *self.sems, self.base + 1 + d, h["y_mates"][d])
            for d in range(3)
        ]

    def add_ring(self):
        k, y = self.here["k"], self.here["y"]
        self.total[4 * k + y] = (self.half[y] + self.parts[0]) + (self.parts[1] + self.parts[2])

    def third(self):
        h = self.here
        slot = self.total.at[4 * h["k"] + h["y"]]
        return [remote(slot, slot, *self.sems, self.base + 4 + d, h["y_mates"][d]) for d in range(3)]

    def fourth(self):
        group = self.total.at[pl.ds(4 * self.here["k"], 4)]
        return [remote(group, group, *self.sems, self.base + 7, self.here["mate"])]

    def unpack(self, store):
        for n, (i, j) in enumerate(PAIRS):
            done = 0
            while done < T:
                q, o = divmod(n * T + done, PIECE)
                m = min(T - done, PIECE - o)
                store(i * T + done, m, j * T, self.total[q, o : o + m, :])
                done += m


def start(copies):
    for cp in copies:
        cp.start()


def wait(copies):
    for cp in copies:
        cp.wait()


def step_kernel(
    panel_ref, trail_ref, out_ref, vec_ref,
    r_ref, rit_ref, lui_ref, mi_ref, x_ref, s_ref, e_ref,
    g0, g1, g2, g3, g4, c0, c1, c2, c3, c4,
    top, zp, zo, zh, zparts, zc, zs, xs, sx0, sx1, rx0, rx1, az0, az1, ax0, ax1, py, pc, qc,
    k2t, img, wr, vc, yct, cc, sends, recvs,
):
    r, c = lax.axis_index("row"), lax.axis_index("col")
    y, k = lax.div(r, 2), lax.rem(r, 2)
    x, z = lax.div(c, 4), lax.rem(c, 4)
    ys = [lax.rem(y + d, 4) for d in range(1, 4)]
    mate = (2 * y + 1 - k, c)
    y_mates = [(2 * v + k, c) for v in ys]
    y_cross = [(2 * v + 1 - k, c) for v in ys]
    x_mates = [(r, lax.rem(x + d, 4) * 4 + z) for d in range(1, 4)]
    z_mates = [(r, x * 4 + lax.rem(z + d, 4)) for d in range(1, 4)]
    peers = [mate] + y_mates + y_cross + x_mates + z_mates
    sems = (sends, recvs)
    here = {"k": k, "y": y, "ys": ys, "mate": mate, "y_mates": y_mates}
    to_r, to_c = lax.div(c, 2), 8 * lax.rem(c, 2) + r
    from_r, from_c = lax.rem(c, 8), 2 * r + lax.div(c, 8)
    fixed = (to_r == r) & (to_c == c)

    barrier = pltpu.get_barrier_semaphore()
    for peer in peers:
        pl.semaphore_signal(barrier, inc=1, device_id=peer, device_id_type=MESH)

    @pl.when(jnp.logical_not(fixed))
    def _():
        pl.semaphore_signal(barrier, inc=1, device_id=(from_r, from_c), device_id_type=MESH)


    gram = Sum((g0, g1, g2, g3, g4), sems, 0, here)
    curv = Sum((c0, c1, c2, c3, c4), sems, 8, here)
    TOP, ZRS, ZAG, PERM, XSC, AXA, AXB, AZA, AZB, PAN, QQ = 16, 24, 28, 32, 33, 37, 43, 49, 55, 61, 69
    FAN = 76

    gram.fill(lambda i: dot_t(panel_ref[:, i * T : (i + 1) * T], panel_ref[:, i * T :]))

    pl.semaphore_wait(barrier, len(peers) + jnp.where(fixed, 0, 1))

    def top_out():
        out = []
        for n, peer in enumerate([(1, c)] + [(2 * v + q, c) for v in range(1, 4) for q in range(2)]):
            q = 1 if n == 0 else (n - 1) % 2
            place = x + 4 * z if q == 0 else z + 4 * x
            out.append(pltpu.make_async_remote_copy(
                src_ref=panel_ref.at[pl.ds(pl.multiple_of(32 * c + 16 * q, 16), 16)],
                dst_ref=top.at[q, place], send_sem=sends.at[FAN + n], recv_sem=recvs.at[TOP],
                device_id=peer, device_id_type=MESH))
        return out

    mine = jnp.where(k == 0, x + 4 * z, z + 4 * x)

    def top_spread(base, src, peers_0, peers_1):
        return [
            remote(src, src, sends, recvs, base + d, (r, jnp.where(k == 0, peers_0[d][1], peers_1[d][1])))
            for d in range(3)
        ]

    top_a = lambda: top_spread(TOP + 1, top.at[k, mine], x_mates, z_mates)
    top_b = lambda: top_spread(TOP + 4, top.at[k, pl.ds(4 * jnp.where(k == 0, z, x), 4)], z_mates, x_mates)
    top_c = lambda: [remote(top.at[k], top.at[k], sends, recvs, TOP + 7, mate)]

    def scatter_first():
        out = []
        for d in range(3):
            out.append(pltpu.make_async_remote_copy(
                src_ref=sx0.at[d + 1], dst_ref=rx0, send_sem=sends.at[FAN + 7 + d], recv_sem=recvs.at[XSC],
                device_id=(r, d + 1), device_id_type=MESH))
            out.append(pltpu.make_async_remote_copy(
                src_ref=sx1.at[d + 1], dst_ref=rx1, send_sem=sends.at[FAN + 10 + d], recv_sem=recvs.at[XSC + 1],
                device_id=(r, 4 * (d + 1)), device_id_type=MESH))
        return out

    def scatter_second(axis):
        out = []
        for d in range(3):
            src, dst, to = (rx0, 0, 4 * (d + 1) + z) if axis == 0 else (rx1, 32, 4 * x + d + 1)
            out.append(pltpu.make_async_remote_copy(
                src_ref=src.at[d + 1], dst_ref=xs.at[pl.ds(dst, 32)], send_sem=sends.at[FAN + 13 + 3 * axis + d],
                recv_sem=recvs.at[XSC + 2 + axis], device_id=(r, to), device_id_type=MESH))
        return out

    def scatter_relay():
        @pl.when((x == 0) & (z > 0))
        def _():
            remote(rx0, rx0, sends, recvs, XSC, mate).wait_recv()

        @pl.when((z == 0) & (x > 0))
        def _():
            remote(rx1, rx1, sends, recvs, XSC + 1, mate).wait_recv()

        @pl.when(x == 0)
        def _():
            start(scatter_second(0))
            xs[0:32, :] = rx0[0]

        @pl.when(z == 0)
        def _():
            start(scatter_second(1))
            xs[32:64, :] = rx1[0]

    def scatter_arrived():
        @pl.when(x > 0)
        def _():
            remote(rx0.at[0], rx0.at[0], sends, recvs, XSC + 2, mate).wait_recv()

        @pl.when(z > 0)
        def _():
            remote(rx1.at[0], rx1.at[0], sends, recvs, XSC + 3, mate).wait_recv()

    def gather_a(src, h0, h1, base):
        return [remote(src.at[pl.ds(0, 32)], h0.at[4 * z + x], sends, recvs, base + d, x_mates[d]) for d in range(3)] + [
            remote(src.at[pl.ds(32, 32)], h1.at[4 * x + z], sends, recvs, base + 3 + d, z_mates[d]) for d in range(3)]

    def gather_own(src, h0, h1):
        h0[4 * z + x] = src[0:32, :]
        h1[4 * x + z] = src[32:64, :]

    def gather_b(h0, h1, base):
        g0_, g1_ = h0.at[pl.ds(4 * z, 4)], h1.at[pl.ds(4 * x, 4)]
        return [remote(g0_, g0_, sends, recvs, base + d, z_mates[d]) for d in range(3)] + [
            remote(g1_, g1_, sends, recvs, base + 3 + d, x_mates[d]) for d in range(3)]

    def z_first():
        return [remote(zp.at[pl.ds(4 * (1 - k), 4)], zo, sends, recvs, ZRS, mate)]

    def z_second():
        return [remote(zh.at[ys[d]], zparts.at[d], sends, recvs, ZRS + 1 + d, y_mates[d]) for d in range(3)]

    def z_third():
        slot = zc.at[y, k]
        return [remote(slot, slot, sends, recvs, ZAG + d, y_mates[d]) for d in range(3)]

    def z_fourth():
        return [remote(zc.at[:, k], zc.at[:, k], sends, recvs, ZAG + 3, mate)]

    def z_move():
        return remote(zc.at[y, k], zs, sends, recvs, PERM, (to_r, to_c))

    def block_first(src_half, dst, base, at_y, at_k):
        return remote(src_half, dst.at[1 - at_k], sends, recvs, base, mate)

    def block_second(dst, base, at_y):
        return [remote(dst.at[k], dst.at[k], sends, recvs, base + 1 + d, y_mates[d]) for d in range(3)]

    def block_third(dst, base):
        return [remote(dst.at[k], dst.at[k], sends, recvs, base + 4, mate)]

    giver = k == lax.div(z, 2)
    given = 512 * lax.rem(z, 2)

    def pan_first():
        out = []
        for d in range(3):
            for q, peer in ((0, (2 * ys[d], c)), (1, (2 * ys[d] + 1, c))):
                out.append(pltpu.make_async_remote_copy(
                    src_ref=panel_ref.at[pl.ds(pl.multiple_of(given + 128 * x + 64 * q, 64), 64)],
                    dst_ref=py.at[d], send_sem=sends.at[FAN + 22 + 2 * d + q], recv_sem=recvs.at[PAN + d],
                    device_id=peer, device_id_type=MESH))
        return out

    def pan_first_arrived():
        for d in range(3):
            remote(py.at[d], py.at[d], sends, recvs, PAN + d, mate).wait_recv()

    def pan_second(act):
        for d in range(3):
            xt = lax.rem(x + d + 1, 4)

            @pl.when(xt != y)
            def _():
                act(remote(py.at[lax.rem(y - xt + 4, 4) - 1], pc.at[k, x], sends, recvs, PAN + 3 + d, (r, 4 * xt + z)))

    def pan_third(q, n):
        return remote(pc.at[q], pc.at[q], sends, recvs, PAN + 6 + n, mate)

    start(gram.first())
    pl.when(r == 0)(lambda: start(top_out()))

    @pl.when(r == 0)
    def _():
        block_first(trail_ref.at[pl.ds(256, 256)], qc, QQ, 0, 0).start()
        qc[0] = trail_ref[0:256, :]
        top[0, x + 4 * z] = panel_ref[pl.ds(pl.multiple_of(32 * c, 32), 16), :]

    @pl.when(c == 0)
    def _():
        for n in range(16):
            sx0[n % 4, n // 4] = trail_ref[64 * n : 64 * n + 32, :]
            sx1[n // 4, n % 4] = trail_ref[64 * n + 32 : 64 * n + 64, :]
        start(scatter_first())
        rx0[...] = sx0[0]
        rx1[...] = sx1[0]

    wait(gram.first())
    gram.add_pair()
    start(gram.second())

    for half in range(2):
        acc = None
        for q in range(4):
            left = trail_ref[256 * q : 256 * (q + 1), 256 * half : 256 * (half + 1)].T
            term = dot3(left, panel_ref[256 * q : 256 * (q + 1), :])
            acc = term if acc is None else acc + term
        for q in range(4):
            s = 4 * half + q
            zp[4 * (s % 2) + s // 2] = acc[64 * q : 64 * (q + 1), :]
    start(z_first())

    @pl.when(r > 0)
    def _():
        remote(top.at[k, mine], top.at[k, mine], sends, recvs, TOP, mate).wait_recv()

    start(top_a())
    wait(gram.second())
    gram.add_ring()
    start(gram.third())
    wait(z_first())
    zh[...] = zp[pl.ds(4 * k, 4)] + zo[...]
    wait(top_a())
    start(top_b())
    scatter_relay()
    wait(gram.third())
    start(gram.fourth())
    start(z_second())
    pl.when(giver)(lambda: start(pan_first()))
    wait(gram.fourth())

    def put(i, m, j, v):
        x_ref[i : i + m, j : j + T] = v

    gram.unpack(put)
    wait(top_b())
    start(top_c())

    scatter_arrived()
    gather_own(xs, ax0, ax1)
    start(gather_a(xs, ax0, ax1, AXA))

    def mid0():
        wait(z_second())
        zc[y, k] = (zh[y] + zparts[0]) + (zparts[1] + zparts[2])

        @pl.when(fixed)
        def _():
            zs[...] = zc[y, k]

        @pl.when(jnp.logical_not(fixed))
        def _():
            z_move().start()

        start(z_third())

    def hook0():
        wait(top_c())
        for a in range(4):
            for b in range(4):
                s_ref[32 * (4 * a + b) : 32 * (4 * a + b) + 16, :] += top[0, a + 4 * b]
                s_ref[32 * (4 * a + b) + 16 : 32 * (4 * a + b) + 32, :] += top[1, b + 4 * a]

    def mid1():
        wait(gather_a(xs, ax0, ax1, AXA))
        start(gather_b(ax0, ax1, AXB))

    def hook1():
        @pl.when(jnp.logical_not(fixed))
        def _():
            z_move().wait()

        gather_own(zs, az0, az1)
        start(gather_a(zs, az0, az1, AZA))

    def mid2():
        pan_first_arrived()
        pan_second(lambda cp: cp.start())

        @pl.when(x != y)
        def _():
            pc[k, x] = py[lax.rem(y - x + 4, 4) - 1]

        @pl.when((x == y) & giver)
        def _():
            for q in range(4):
                for h in range(2):
                    pc[h, q] = panel_ref[pl.ds(pl.multiple_of(given + 128 * q + 64 * h, 64), 64), :]
            pan_third(k, 0).start()
            pan_third(1 - k, 1).start()

        @pl.when(y == 0)
        def _():
            @pl.when(k != 0)
            def _():
                block_first(trail_ref.at[pl.ds(256, 256)], qc, QQ, 0, 0).wait_recv()

            start(block_second(qc, QQ, 0))

    def hook2():
        wait(z_third())
        start(z_fourth())

    def mid3():
        wait(gather_a(zs, az0, az1, AZA))
        start(gather_b(az0, az1, AZB))

    def hook4():
        @pl.when(x != y)
        def _():
            for d in range(3):
                remote(pc.at[k, 0], pc.at[k, 0], sends, recvs, PAN + 3 + d, mate).wait_recv()
            pan_third(k, 0).start()

    def block_arrive(dst, base, at_y):
        @pl.when(y == at_y)
        def _():
            for cp in block_second(dst, base, at_y):
                cp.wait_send()

        @pl.when(y != at_y)
        def _():
            for d in range(3):
                @pl.when(lax.rem(at_y + d + 1, 4) == y)
                def _():
                    block_second(dst, base, at_y)[d].wait_recv()

        start(block_third(dst, base))

    def hook6():
        wait(z_fourth())
        wait(gather_b(ax0, ax1, AXB))
        pan_second(lambda cp: cp.wait_send())

        @pl.when(x != y)
        def _():
            pan_third(k, 0).wait()

        @pl.when((x == y) & giver)
        def _():
            pan_third(k, 0).wait_send()
            pan_third(1 - k, 1).wait_send()

        @pl.when((x == y) & jnp.logical_not(giver))
        def _():
            pan_third(1 - k, 0).wait_recv()
            pan_third(k, 1).wait_recv()

    def hook8():
        block_arrive(qc, QQ, 0)

        @pl.when(giver)
        def _():
            for cp in pan_first():
                cp.wait_send()

        @pl.when(r == 0)
        def _():
            for cp in top_out():
                cp.wait_send()
            block_first(trail_ref.at[pl.ds(256, 256)], qc, QQ, 0, 0).wait_send()

        @pl.when(c == 0)
        def _():
            for cp in scatter_first():
                cp.wait_send()

        @pl.when(x == 0)
        def _():
            for cp in scatter_second(0):
                cp.wait_send()

        @pl.when(z == 0)
        def _():
            for cp in scatter_second(1):
                cp.wait_send()


    mids = {0: mid0, 1: mid1, 2: mid2}
    hooks = {0: hook0, 1: hook1, 2: hook2, 3: mid3, 4: hook4, 6: hook6, 8: hook8}
    r_i = lax.broadcasted_iota(jnp.int32, (B, B), 0)
    c_i = lax.broadcasted_iota(jnp.int32, (B, B), 1)
    eye = (r_i == c_i).astype(jnp.float32)
    s_ref[...] = jnp.zeros_like(s_ref)
    r_ref[...] = jnp.zeros_like(r_ref)
    rit_ref[...] = jnp.zeros_like(rit_ref)
    lui_ref[...] = jnp.zeros_like(lui_ref)
    mi_ref[...] = jnp.zeros_like(mi_ref)
    for t in range(3):
        e_ref[t, :, :B] = eye
        e_ref[t, :, B:] = eye

    def diag(v):
        return jnp.sum(jnp.where(r_i == c_i, v, 0.0), axis=1, keepdims=True)

    def pre(p):
        a, b = p * B, (p + 1) * B
        if p < NPH:
            block = x_ref[a:b, a:b]
            e_ref[0, :, :B] = jnp.where(r_i <= c_i, block, block.T)
            e_ref[0, :, B:] = eye
        if p > 0:
            a, b = a - B, b - B
            block = s_ref[a:b, a:b]
            e_ref[1, :, :B] = block
            e_ref[1, :, B:] = eye
            e_ref[2, :, :B] = block.T
            e_ref[2, :, B:] = eye

    def post(p):
        a, b = p * B, (p + 1) * B
        if p < NPH:
            left = e_ref[0, :, :B]
            rs = lax.rsqrt(diag(left))
            linv = rs * e_ref[0, :, B:]
            rpp = jnp.where(r_i <= c_i, rs * left, 0.0)
            r_ref[a:b, a:b] = rpp
            rit_ref[a:b, a:b] = linv
            if p:
                rit_ref[a:b, :a] = dot3(linv, rit_ref[a:b, :a])
            s_ref[a:b, a:b] += rpp
            if b < NB:
                rrow = dot(linv, x_ref[a:b, b:])
                r_ref[a:b, b:] = rrow
                s_ref[a:b, b:] += rrow
                x_ref[b:, b:] -= dot_t(rrow, rrow)
                rit_ref[b:, :b] -= dot3(rrow.T, rit_ref[a:b, :b])
        if p > 0:
            a, b = a - B, b - B
            lui = e_ref[1, :, B:]
            mit = (1.0 / diag(e_ref[2, :, :B])) * e_ref[2, :, B:]
            mi = mit.T
            lui_ref[a:b, a:b] = lui
            mi_ref[a:b, a:b] = mi
            if a:
                lui_ref[a:b, :a] = dot3(lui, lui_ref[a:b, :a])
                mi_ref[:a, a:b] = dot3(mi_ref[:a, a:b], mi)
            if b < NB:
                mrow = dot(lui, s_ref[a:b, b:])
                lucol = dot(s_ref[b:, a:b], mi)
                s_ref[b:, b:] -= dot(lucol, mrow)
                lui_ref[b:, :b] -= dot3(lucol, lui_ref[a:b, :b])
                mi_ref[:b, b:] -= dot3(mi_ref[:b, a:b], mrow)

    def phase(ph, carry):
        for p in range(NPH + 1):
            pl.when(ph == p)(functools.partial(pre, p))
        eliminate(e_ref, 3)
        for p, hook in mids.items():
            pl.when(ph == p)(hook)
        for p in range(NPH + 1):
            pl.when(ph == p)(functools.partial(post, p))
        for p, hook in hooks.items():
            pl.when(ph == p)(hook)
        return carry

    lax.fori_loop(0, NPH + 1, phase, 0)


    k2t[...] = dot3(lui_ref[...], rit_ref[...])
    k2 = split(k2t[...])
    lui = split(lui_ref[...])
    def shifted(q):
        block = panel_ref[256 * q : 256 * (q + 1), :]
        if q < 2:
            block = block + jnp.where(r == 0, r_ref[256 * q : 256 * (q + 1), :], 0.0)
        return block

    for q in range(4):
        wr[256 * q : 256 * (q + 1), :] = dot3(shifted(q), k2, NT)
    wait(gather_b(az0, az1, AZB))
    for az, ax, h in ((az0, ax0, 0), (az1, ax1, 1)):
        val = dot3(az[...].reshape(NB, NB), k2, NT) + dot3(ax[...].reshape(NB, NB), lui, NT)
        for n in range(16):
            j = 4 * (n % 4) + n // 4 if h == 0 else n
            img[64 * j + 32 * h : 64 * j + 32 * h + 32, :] = val[32 * n : 32 * n + 32, :]

    curv.fill(lambda i: dot3(wr[:, i * T : (i + 1) * T].T, img[:, i * T :]))
    start(curv.first())
    mi = split(mi_ref[...])
    for q in range(4):
        for h in range(2):
            rows = pl.ds(128 * q + 64 * h, 64)
            vc[rows, :] = pc[h, q] + jnp.where(c == 0, r_ref[rows, :], 0.0)
    vc[...] = dot3(vc[...], mi)
    wait(curv.first())
    curv.add_pair()
    start(curv.second())
    for q in range(4):
        vec_ref[256 * q : 256 * (q + 1), :] = dot3(shifted(q), mi)
    wait(curv.second())
    curv.add_ring()
    start(curv.third())
    wait(block_third(qc, QQ))
    yct[...] = dot3(k2, zc[...].reshape(NB, NB), NT) + dot3(lui, qc[...].reshape(NB, NB))
    wait(curv.third())
    start(curv.fourth())
    vcs = split(vc[...])
    for q in range(4):
        rows = pl.ds(256 * q, 256)
        out_ref[rows, :] = trail_ref[rows, :] - dot3(img[rows, :], vcs, NT)
    wait(curv.fourth())

    def put_c(i, m, j, v):
        cc[i : i + m, j : j + T] = v
        if i // T * T != j:
            cc[j : j + T, i : i + m] = v.T

    curv.unpack(put_c)
    dct = split(yct[...] - dot3(cc[...], vcs, NT))
    for q in range(4):
        rows = pl.ds(256 * q, 256)
        out_ref[rows, :] -= dot3(vec_ref[rows, :], dct)


def on_device(panel, trailing):
    f32 = jnp.float32
    vm = pl.BlockSpec(memory_space=pltpu.VMEM)
    sq = pltpu.VMEM((NB, NB), f32)
    sums = [(8, PIECE, T), (4, PIECE, T), (4, PIECE, T), (3, PIECE, T), (8, PIECE, T)]
    shapes = [(NB, NB)] * 6 + [(3, B, 2 * B)] + sums * 2 + [
        (2, 16, 16, NB),
        (8, 64, NB), (4, 64, NB), (4, 64, NB), (3, 64, NB), (4, 2, 64, NB),
        (64, NB), (64, NB), (4, 4, 32, NB), (4, 4, 32, NB), (4, 32, NB), (4, 32, NB),
        (16, 32, NB), (16, 32, NB), (16, 32, NB), (16, 32, NB),
        (3, 64, NB), (2, 4, 64, NB), (2, 256, NB),
        (NB, NB), (1024, NB), (1024, NB), (NB, NB), (NB, NB), (NB, NB),
    ]
    return tuple(pl.pallas_call(
        step_kernel,
        out_shape=[jax.ShapeDtypeStruct((1024, NB), f32)] * 2,
        in_specs=[vm] * 2,
        out_specs=[vm] * 2,
        scratch_shapes=[pltpu.VMEM(s, f32) for s in shapes]
        + [pltpu.SemaphoreType.DMA((108,)), pltpu.SemaphoreType.DMA((76,))],
        compiler_params=pltpu.CompilerParams(
            vmem_limit_bytes=56 * 1024 * 1024, collective_id=0, has_side_effects=True),
        name="step",
    )(panel, trailing))


def solution(mesh):
    return jax.shard_map(
        on_device,
        mesh=mesh,
        in_specs=(P("row", None), P("row", "col")),
        out_specs=(P("row", "col"), P("row", None)),
        check_vma=False,
    )
```
